32 devices in a mesh: groups: 2 (over x), row: 8 (over z, y), col: 2 (over core).
Axes of the slice: x: 2, y: 2, z: 4, core: 2. Of those that a mesh axis runs over, the one named last changes fastest.
Arguments:
- a_values: bfloat16 [64, 8, 2, 128, 128], P(('groups', 'col'), 'row'), parts along dimension 0, may hold values from -6 to 6
- a_index: int32 [64, 8, 2], P(('groups', 'col'), 'row'), parts along dimension 0, may hold values from -1 to 3
- b_values: bfloat16 [64, 8, 4, 128, 128], P(('groups', 'col'), 'row'), parts along dimension 0, may hold values from -0.125 to 0.125
- b_index: int32 [64, 8, 4], P(('groups', 'col'), 'row'), parts along dimension 0, may hold values from -1 to 7
Outputs:
- product: bfloat16 [64, 8, 8, 128, 128], P(('groups', 'col'), 'row'), parts along dimension 0
The draws below stay inside these ranges and needn't reach their ends.
There are 2 independent parts, one for each index of `groups`. The reference program is written for one: setup_inputs(seed, part) draws one part's arguments, and reference() takes and returns one part's arrays. A program takes and returns all parts, laid end to end along the dimension named above; each array names one. Nothing has to cross between parts.
Inputs may be any that keep to these rules, and one draw needn't show every extreme that they name: `a_index`: a value of -1 marks an empty slot. `b_index`: a value of -1 marks an empty slot.
All inputs are finite; a program needn't handle non-finite values.
Results may differ from the reference program's by a relative error of at most 0.0034.
Values may be sent and summed in bfloat16 or wider, within the bound.
No kernel may reach another device: no remote copies, remote signals or barrier semaphores. Data moves between devices by JAX's collectives and lax.ppermute only.
A program may use at most 320 MiB of HBM per device.

```python
import jax
import jax.numpy as jnp
from jax import lax

BLK = 128
SA = 2
BK = 4
BJ = 8
SB = 4
ROWS_I = 32
NK = 32
N_ROW = 8


def set_ends(result, stream_key, low, high):
    extent = result.shape
    spot = [jax.random.randint(jax.random.fold_in(stream_key, axis), (), 0, extent[axis]) for axis in range(len(extent))]
    result = result.at[tuple(spot)].set(low)
    longest = extent.index(max(extent))
    spot[longest] = (spot[longest] + 1) % extent[longest]
    return result.at[tuple(spot)].set(high)


def block_scale(key, dims, cuts, least, top_value):
    level = 1.0
    for dim, shards_of in cuts:
        steps = jax.random.uniform(jax.random.fold_in(jax.random.fold_in(key, 6), dim), (shards_of,), jnp.float32, least / len(cuts), top_value / len(cuts))
        level = level * jnp.repeat(jnp.exp(steps), dims[dim] // shards_of).reshape((-1,) + (1,) * (len(dims) - 1 - dim))
    return level


def gaussian(rng, shape, deviation, reach, cuts=(), held_as=jnp.bfloat16):
    factor_of = block_scale(rng, shape, cuts, -0.22, 0.18) if cuts else 1.0
    array = jax.random.normal(rng, shape, jnp.float32) * deviation * factor_of
    return jnp.minimum(jnp.maximum(array, -reach), reach).astype(held_as)


def setup_inputs(seed: int = 0, part: int = 0) -> dict:
    key_of = jax.random.split(jax.random.key(seed), 5)
    own_keys = jax.random.split(jax.random.fold_in(key_of[4], part), 5)
    a_values = gaussian(own_keys[0], (ROWS_I, N_ROW, SA, BLK, BLK), 1.0, 6.0, ((0, 2), (1, 8)))
    a_index = set_ends(jax.random.randint(own_keys[1], (ROWS_I, N_ROW, SA), -1, BK), jax.random.fold_in(own_keys[1], 1), -1, BK - 1).astype(jnp.int32)
    b_values = gaussian(own_keys[2], (NK, N_ROW, SB, BLK, BLK), (BLK * N_ROW * SA) ** -0.5, 0.125, ((0, 2), (1, 8)))
    b_index = set_ends(jax.random.randint(own_keys[3], (NK, N_ROW, SB), -1, BJ), jax.random.fold_in(own_keys[3], 1), -1, BJ - 1).astype(jnp.int32)
    return dict(a_values=a_values, a_index=a_index, b_values=b_values, b_index=b_index)


def reference(a_values, a_index, b_values, b_index):
    columns = jnp.arange(BJ, dtype=jnp.int32)
    onehot = (b_index[:, :, :, None] == columns).astype(jnp.float32)
    right_dense = jnp.einsum("krsw,krsxy->krwxy", onehot, b_values.astype(jnp.float32), precision=lax.Precision.HIGHEST).astype(jnp.bfloat16)
    pieces = jnp.arange(N_ROW, dtype=jnp.int32)

    def one_row(inputs):
        values, index = inputs
        valid = index >= 0
        inner = jnp.where(valid, pieces[:, None] * BK + index, 0).astype(jnp.int32)
        chosen = right_dense[inner].astype(jnp.float32)
        masked = values.astype(jnp.float32) * valid[:, :, None, None].astype(jnp.float32)
        total = jnp.einsum("psxy,psrjyz->rjxz", masked, chosen, precision=lax.Precision.HIGHEST)
        return total.astype(jnp.bfloat16)

    return lax.map(one_row, (a_values, a_index))
```

```python
import functools

import jax
import jax.numpy as jnp
import numpy as np
from jax import lax
from jax.experimental import pallas as pl
from jax.experimental.pallas import tpu as pltpu
from jax.sharding import PartitionSpec as P

BJ = 8
VMEM_LIMIT = 20 * 1024 * 1024


def ring_order(n):
    if n == 8:
        return (0, 2, 4, 6, 7, 5, 3, 1)
    return tuple(range(n))


def densify_kernel(col_ref, own_index, other_index, own_ref, other_ref, dense_ref):
    source = pl.program_id(0)
    first = pl.program_id(1) * own_ref.shape[0]
    blk = own_ref.shape[-1]
    slots = own_ref.shape[1]
    for k in range(own_ref.shape[0]):
        stored = [
            jnp.where(source == 0, own_ref[k, t], other_ref[k, t]).astype(jnp.float32)
            for t in range(slots)
        ]
        at = [(first + k) * slots + t for t in range(slots)]
        columns = [jnp.where(source == 0, own_index[i], other_index[i]) for i in at]
        for j in range(BJ):
            total = jnp.zeros((blk, blk), jnp.float32)
            for t in range(slots):
                total = total + jnp.where(columns[t] == j, stored[t], 0.0)
            dense_ref[0, k, :, j * blk : (j + 1) * blk] = total.astype(jnp.bfloat16)


def densify(col, own_index, other_index, own, other, pieces, inner_width):
    slots, blk = own.shape[1], own.shape[-1]
    stored = (inner_width, slots, blk, blk)
    return pl.pallas_call(
        densify_kernel,
        out_shape=jax.ShapeDtypeStruct((2 * pieces, inner_width, blk, BJ * blk), jnp.bfloat16),
        grid_spec=pltpu.PrefetchScalarGridSpec(
            num_scalar_prefetch=3,
            grid=(2, pieces),
            in_specs=[
                pl.BlockSpec(stored, lambda s, g, c, *i: (jnp.where(s == 0, g, pieces - 1), 0, 0, 0)),
                pl.BlockSpec(stored, lambda s, g, c, *i: (jnp.where(s == 0, 0, g), 0, 0, 0)),
            ],
            out_specs=pl.BlockSpec(
                (1, inner_width, blk, BJ * blk),
                lambda s, g, c, *i: (jnp.where(s == 0, c[0], 1 - c[0]) * pieces + g, 0, 0, 0),
            ),
        ),
        compiler_params=pltpu.CompilerParams(vmem_limit_bytes=VMEM_LIMIT),
        cost_estimate=pl.CostEstimate(
            flops=2 * pieces * inner_width * slots * BJ * blk * blk * 2,
            bytes_accessed=2 * own.size * 2 + 2 * pieces * inner_width * BJ * blk * blk * 2,
            transcendentals=0,
        ),
    )(col, own_index, other_index, own, other)


def product_kernel(offsets, sides, starts, has_total, last, step, *refs):
    count = len(offsets)
    index = refs[1 : 1 + count]
    refs = refs[1 + count :]
    left = refs[: count * sides]
    right = refs[count * sides : count * (sides + 1)]
    rest = refs[count * (sides + 1) :]
    out_ref = rest[-1]
    total_ref = rest[0] if has_total else None
    slots, blk = left[0].shape[1], left[0].shape[-1]
    wide = 2 * blk
    g = pl.program_id(0)
    if sides == 2:
        each = pl.num_programs(0) // 2
        second = g >= each
        row0 = jnp.where(second, starts[1] + (g - each) * step, starts[0] + g * step)
    else:
        row0 = starts[0] + g * step
    for i in range(step):
        factors = []
        for m in range(count):
            inner = [index[m][(row0 + i) * slots + s] for s in range(slots)]
            parts = []
            for s in range(slots):
                part = left[m * sides][i, s]
                if sides == 2:
                    part = jnp.where(second, left[m * sides + 1][i, s], part)
                parts.append(jnp.where(inner[s] >= 0, part, jnp.zeros((), jnp.bfloat16)))
            factors.append((jnp.concatenate(parts, axis=1), [jnp.maximum(k, 0) for k in inner]))
        for c in range(BJ // 2):
            columns = slice(c * wide, (c + 1) * wide)
            total = total_ref[i, :, columns] if has_total else None
            for m in range(count):
                row, inner = factors[m]
                rows_of = jnp.concatenate([right[m][0, k, :, columns] for k in inner], axis=0)
                term = jnp.dot(row, rows_of, preferred_element_type=jnp.float32)
                total = term if total is None else total + term
            if last:
                for j in range(2):
                    out_ref[i, 0, c * 2 + j] = total[:, j * blk : (j + 1) * blk].astype(jnp.bfloat16)
            else:
                out_ref[i, :, columns] = total


def product(cycle, offsets, index, left, right, total, starts, rows, target=None, last=False, step=2):
    count, sides = len(offsets), len(starts)
    size, slots, blk, _ = left[0][0].shape
    step = min(step, size)
    each = size // step
    inner_width = right.shape[1]

    def of_side(s):
        if s == 0:
            return lambda g, *p: (jnp.minimum(g, each - 1), 0, 0, 0)
        return lambda g, *p: (jnp.maximum(g - each, 0), 0, 0, 0)

    def place(g):
        if sides == 1:
            return starts[0] // step + g
        return jnp.where(g < each, starts[0] // step + g, starts[1] // step + g - each)

    in_specs = [
        pl.BlockSpec((step, slots, blk, blk), of_side(s)) for _ in range(count) for s in range(sides)
    ]
    in_specs += [
        pl.BlockSpec(
            (1, inner_width, blk, BJ * blk), functools.partial(lambda o, g, c, *p: (c[o], 0, 0, 0), o)
        )
        for o in offsets
    ]
    operands = [cycle, *index, *(array for piece in left for array in piece), *([right] * count)]
    aliases = {}
    if total is not None:
        in_specs.append(pl.BlockSpec((step, blk, BJ * blk), lambda g, *p: (place(g), 0, 0)))
        operands.append(total)
        if not last:
            aliases = {len(operands) - 1: 0}
    if target is not None:
        in_specs.append(pl.BlockSpec(memory_space=pl.ANY))
        operands.append(target)
        aliases = {len(operands) - 1: 0}
    if last:
        out_shape = jax.ShapeDtypeStruct((rows, 1, BJ, blk, blk), jnp.bfloat16)
        out_spec = pl.BlockSpec((step, 1, BJ, blk, blk), lambda g, *p: (place(g), 0, 0, 0, 0))
    else:
        out_shape = jax.ShapeDtypeStruct((rows, blk, BJ * blk), jnp.float32)
        out_spec = pl.BlockSpec((step, blk, BJ * blk), lambda g, *p: (place(g), 0, 0))
    wide = BJ * blk * blk * size * sides
    return pl.pallas_call(
        functools.partial(
            product_kernel, offsets, sides, starts, total is not None, last, step
        ),
        out_shape=out_shape,
        grid_spec=pltpu.PrefetchScalarGridSpec(
            num_scalar_prefetch=1 + count,
            grid=(each * sides,),
            in_specs=in_specs,
            out_specs=out_spec,
        ),
        input_output_aliases=aliases,
        compiler_params=pltpu.CompilerParams(vmem_limit_bytes=VMEM_LIMIT),
        cost_estimate=pl.CostEstimate(
            flops=2 * wide * blk * slots * count,
            bytes_accessed=wide * (2 if last else 4)
            + (wide * 4 if total is not None else 0)
            + count * (size * sides * slots + inner_width * BJ) * blk * blk * 2,
            transcendentals=0,
        ),
    )(*operands)


def body(a_values, a_index, b_values, b_index):
    n = lax.axis_size("row")
    order = ring_order(n)
    ahead = [(order[q], order[(q + 1) % n]) for q in range(n)]
    back = [(dst, src) for src, dst in ahead]
    whole_steps = n // 2 - 1
    rows, _, slots, blk, _ = a_values.shape
    half = rows // 2

    swap = [(0, 1), (1, 0)]
    own = (a_values[:, 0], a_index.reshape(-1))
    from_behind, from_ahead = [own], [own]

    def advance():
        behind, ahead_of = from_behind[-1], from_ahead[-1]
        from_behind.append(tuple(lax.ppermute(x, "row", ahead) for x in behind[::-1])[::-1])
        from_ahead.append(tuple(lax.ppermute(x, "row", back) for x in ahead_of[::-1])[::-1])

    advance()
    col = lax.axis_index("col")
    stored, stored_index = b_values[:, 0], b_index.reshape(-1)
    other = lax.ppermute(stored, "col", swap)
    other_index = lax.ppermute(stored_index, "col", swap)
    inner_width = 2 * stored.shape[0] // n
    right = densify(col[None], stored_index, other_index, stored, other, n // 2, inner_width)

    around = np.array([[order[(order.index(r) + o) % n] for o in range(n)] for r in range(n)])
    cycle = lax.dynamic_index_in_dim(
        jnp.asarray(around, jnp.int32), lax.axis_index("row"), 0, keepdims=False
    )

    from_behind[1], from_ahead[1], right = lax.optimization_barrier(
        (from_behind[1], from_ahead[1], right)
    )
    total = None
    for k in range(1, whole_steps + 1):
        if k < whole_steps:
            advance()
        offsets, items = (n - k, k), [from_behind[k], from_ahead[k]]
        if k == 1:
            offsets, items = (0, *offsets), [own, *items]
        if k == whole_steps:
            cuts = [0, half - half // 4, half]
            low = [
                lax.ppermute(from_behind[-1][0][s:e], "row", ahead) for s, e in zip(cuts, cuts[1:])
            ]
            high = [
                lax.ppermute(from_ahead[-1][0][half + s : half + e], "row", back)
                for s, e in zip(cuts, cuts[1:])
            ]
            far_index = lax.ppermute(from_behind[-1][1], "row", ahead)
        index, left = [i for _, i in items], [[v] for v, _ in items]
        total = product(cycle, offsets, index, left, right, total, (0,), rows)
        if k < whole_steps:
            from_behind[-1], from_ahead[-1], total = lax.optimization_barrier(
                (from_behind[-1], from_ahead[-1], total)
            )
    out = None
    for c in range(2):
        starts = (cuts[c], half + cuts[c])
        left = [[low[c], high[c]]]
        out = product(cycle, (n // 2,), [far_index], left, right, total, starts, rows, out, True)
    return out


def solution(mesh):
    placed = (
        P(("groups", "col"), "row", None, None, None),
        P(("groups", "col"), "row", None),
        P(("groups", "col"), "row", None, None, None),
        P(("groups", "col"), "row", None),
    )
    return jax.shard_map(
        body,
        mesh=mesh,
        in_specs=placed,
        out_specs=P(("groups", "col"), "row", None, None, None),
        check_vma=False,
    )
```

```python
import functools

import jax
import jax.numpy as jnp
import numpy as np
from jax import lax
from jax.experimental import pallas as pl
from jax.experimental.pallas import tpu as pltpu
from jax.sharding import PartitionSpec as P

BJ = 8
NOTE_ROWS = 16
VMEM_LIMIT = 20 * 1024 * 1024


def ring_order(n):
    if n == 8:
        return (0, 2, 4, 6, 7, 5, 3, 1)
    return tuple(range(n))


def densify_kernel(col_ref, own_index, other_index, own_ref, other_ref, dense_ref):
    source = pl.program_id(0)
    first = pl.program_id(1) * own_ref.shape[0]
    blk = own_ref.shape[-1]
    slots = own_ref.shape[1]
    for k in range(own_ref.shape[0]):
        stored = [
            jnp.where(source == 0, own_ref[k, t], other_ref[k, t]).astype(jnp.float32)
            for t in range(slots)
        ]
        at = [(first + k) * slots + t for t in range(slots)]
        columns = [jnp.where(source == 0, own_index[i], other_index[i]) for i in at]
        for j in range(BJ):
            total = jnp.zeros((blk, blk), jnp.float32)
            for t in range(slots):
                total = total + jnp.where(columns[t] == j, stored[t], 0.0)
            dense_ref[0, k, :, j * blk : (j + 1) * blk] = total.astype(jnp.bfloat16)


def densify(col, own_index, other_index, own, other, pieces, inner_width):
    slots, blk = own.shape[1], own.shape[-1]
    stored = (inner_width, slots, blk, blk)
    return pl.pallas_call(
        densify_kernel,
        out_shape=jax.ShapeDtypeStruct((2 * pieces, inner_width, blk, BJ * blk), jnp.bfloat16),
        grid_spec=pltpu.PrefetchScalarGridSpec(
            num_scalar_prefetch=3,
            grid=(2, pieces),
            in_specs=[
                pl.BlockSpec(stored, lambda s, g, c, *i: (jnp.where(s == 0, g, pieces - 1), 0, 0, 0)),
                pl.BlockSpec(stored, lambda s, g, c, *i: (jnp.where(s == 0, 0, g), 0, 0, 0)),
            ],
            out_specs=pl.BlockSpec(
                (1, inner_width, blk, BJ * blk),
                lambda s, g, c, *i: (jnp.where(s == 0, c[0], 1 - c[0]) * pieces + g, 0, 0, 0),
            ),
        ),
        compiler_params=pltpu.CompilerParams(vmem_limit_bytes=VMEM_LIMIT),
        name="densify",
        cost_estimate=pl.CostEstimate(flops=0, bytes_accessed=0, transcendentals=0),
    )(col, own_index, other_index, own, other)


def product_kernel(offsets, sides, starts, has_total, step, *refs):
    count = len(offsets)
    index = refs[1 : 1 + count]
    refs = refs[1 + count :]
    left = refs[: count * sides]
    right = refs[count * sides : count * (sides + 1)]
    rest = refs[count * (sides + 1) :]
    out_ref, held = (rest[-2], rest[-1]) if sides == 2 else (rest[-1], None)
    total_ref = rest[0] if has_total else None
    slots, blk = index[0].shape[0], left[0].shape[-1]
    wide = 2 * blk
    g = pl.program_id(0)
    if sides == 2:
        each = pl.num_programs(0) // 2
        second = g >= each
        row0 = jnp.where(second, starts[1] + (g - each) * step, starts[0] + g * step)
    else:
        row0 = starts[0] + g * step
    if sides == 2:
        for m in range(count):

            @pl.when(g < each)
            def _(m=m):
                held[m] = left[m * 2][...]

            @pl.when(g >= each)
            def _(m=m):
                held[m] = left[m * 2 + 1][...]

    for i in range(step):
        factors = []
        for m in range(count):
            inner = [index[m][s, row0 + i] for s in range(slots)]
            parts = []
            for s in range(slots):
                at = slice((i * slots + s) * blk, (i * slots + s + 1) * blk)
                part = left[m][at, :] if sides == 1 else held[m, at, :]
                parts.append(part * jnp.where(inner[s] >= 0, 1.0, 0.0).astype(jnp.bfloat16))
            factors.append((jnp.concatenate(parts, axis=1), [jnp.maximum(k, 0) for k in inner]))
        for c in range(BJ // 2):
            columns = slice(c * wide, (c + 1) * wide)
            total = total_ref[i, :, columns] if has_total else None
            for m in range(count):
                row, inner = factors[m]
                rows_of = jnp.concatenate([right[m][0, k, :, columns] for k in inner], axis=0)
                term = jnp.dot(row, rows_of, preferred_element_type=jnp.float32)
                total = term if total is None else total + term
            out_ref[i, :, columns] = total


def product(cycle, offsets, index, left, right, total, starts, size, rows, step=4):
    count, sides = len(offsets), len(starts)
    slots, blk = index[0].shape[0], left[0][0].shape[-1]
    each = size // step
    inner_width = right.shape[1]

    def of_side(s):
        if s == 0:
            return lambda g, *p: (jnp.minimum(g, each - 1), 0)
        return lambda g, *p: (jnp.maximum(g - each, 0), 0)

    def place(g):
        if sides == 1:
            return starts[0] // step + g
        return jnp.where(g < each, starts[0] // step + g, starts[1] // step + g - each)

    in_specs = [
        pl.BlockSpec((step * slots * blk, blk), of_side(s)) for _ in range(count) for s in range(sides)
    ]
    in_specs += [
        pl.BlockSpec(
            (1, inner_width, blk, BJ * blk), functools.partial(lambda o, g, c, *p: (c[o], 0, 0, 0), o)
        )
        for o in offsets
    ]
    operands = [cycle, *index, *(array for piece in left for array in piece), *([right] * count)]
    aliases = {}
    if total is not None:
        in_specs.append(pl.BlockSpec((step, blk, BJ * blk), lambda g, *p: (place(g), 0, 0)))
        operands.append(total)
        aliases = {len(operands) - 1: 0}
    out_shape = jax.ShapeDtypeStruct((rows, blk, BJ * blk), jnp.float32)
    out_spec = pl.BlockSpec((step, blk, BJ * blk), lambda g, *p: (place(g), 0, 0))
    return pl.pallas_call(
        functools.partial(
            product_kernel, offsets, sides, starts, total is not None, step
        ),
        out_shape=out_shape,
        grid_spec=pltpu.PrefetchScalarGridSpec(
            num_scalar_prefetch=1 + count,
            grid=(each * sides,),
            in_specs=in_specs,
            out_specs=out_spec,
            scratch_shapes=[pltpu.VMEM((count, step * slots * blk, blk), jnp.bfloat16)] * (sides - 1),
        ),
        input_output_aliases=aliases,
        compiler_params=pltpu.CompilerParams(vmem_limit_bytes=VMEM_LIMIT),
        name="product",
        cost_estimate=pl.CostEstimate(flops=0, bytes_accessed=0, transcendentals=0),
    )(*operands)


def finish_kernel(offset, starts, size, cycle, index, low, high, right, total, *refs):
    out_ref, staged, sems = refs[-3:]
    slots, blk = index.shape[0], low.shape[-1]
    wide = 2 * blk
    copies = []
    for half_ref, start in ((low, starts[0]), (high, starts[1])):
        for i in range(size):
            row, at = start + i, len(copies)
            inner = [index[s, row] for s in range(slots)]
            parts = []
            for s in range(slots):
                part = half_ref[(i * slots + s) * blk : (i * slots + s + 1) * blk, :]
                parts.append(part * jnp.where(inner[s] >= 0, 1.0, 0.0).astype(jnp.bfloat16))
            factor = jnp.concatenate(parts, axis=1)
            for c in range(BJ // 2):
                columns = slice(c * wide, (c + 1) * wide)
                rows_of = jnp.concatenate(
                    [right[0, jnp.maximum(k, 0), :, columns] for k in inner], axis=0
                )
                term = jnp.dot(factor, rows_of, preferred_element_type=jnp.float32)
                result = (total[row, :, columns] + term).astype(jnp.bfloat16)
                for j in range(2):
                    staged[at, c * 2 + j] = result[:, j * blk : (j + 1) * blk]
            copies.append(pltpu.make_async_copy(staged.at[at], out_ref.at[row, 0], sems.at[at]))
            copies[-1].start()
    for copy in copies:
        copy.wait()


def finish(cycle, offset, index, low, high, right, total, starts, size, target):
    rows, blk = total.shape[0], total.shape[1]
    inner_width = right.shape[1]
    whole = pl.BlockSpec(memory_space=pltpu.VMEM)
    piece = pl.BlockSpec(
        (1, inner_width, blk, BJ * blk), lambda g, c, *p: (c[offset], 0, 0, 0)
    )
    operands = [cycle, index, low, high, right, total]
    in_specs = [whole, whole, piece, whole]
    aliases = {}
    if target is not None:
        in_specs.append(pl.BlockSpec(memory_space=pl.ANY))
        operands.append(target)
        aliases = {len(operands) - 1: 0}
    return pl.pallas_call(
        functools.partial(finish_kernel, offset, starts, size),
        out_shape=jax.ShapeDtypeStruct((rows, 1, BJ, blk, blk), jnp.bfloat16),
        grid_spec=pltpu.PrefetchScalarGridSpec(
            num_scalar_prefetch=2,
            grid=(1,),
            in_specs=in_specs,
            out_specs=pl.BlockSpec(memory_space=pl.ANY),
            scratch_shapes=[
                pltpu.VMEM((2 * size, BJ, blk, blk), jnp.bfloat16),
                pltpu.SemaphoreType.DMA((2 * size,)),
            ],
        ),
        input_output_aliases=aliases,
        compiler_params=pltpu.CompilerParams(vmem_limit_bytes=VMEM_LIMIT),
        name="finish",
        cost_estimate=pl.CostEstimate(flops=0, bytes_accessed=0, transcendentals=0),
    )(*operands)


def body(a_values, a_index, b_values, b_index):
    n = lax.axis_size("row")
    order = ring_order(n)
    ahead = [(order[q], order[(q + 1) % n]) for q in range(n)]
    back = [(dst, src) for src, dst in ahead]
    whole_steps = n // 2 - 1
    rows, _, slots, blk, _ = a_values.shape
    half = rows // 2

    swap = [(0, 1), (1, 0)]
    flat = a_values.reshape(rows * slots * blk, blk)
    cut = half * slots * blk
    own_index = a_index[:, 0].T
    note = own_index.astype(jnp.bfloat16)
    note = jnp.pad(note, ((0, NOTE_ROWS - slots), (0, blk - rows)))
    low_first, high_second = jnp.concatenate([flat[:cut], note]), flat[cut:]
    high_first, low_second = jnp.concatenate([flat[cut:], note]), flat[:cut]

    def read_note(message):
        return message[-NOTE_ROWS:][:slots, :rows].astype(jnp.int32)

    def move(array, way, name):
        with jax.named_scope(name):
            return lax.ppermute(array, "row", way)

    behind, beyond = [(low_first, high_second)], [(low_second, high_first)]

    def advance():
        low, high = behind[-1]
        far_low, far_high = beyond[-1]
        low, far_high = move(low, ahead, "low_ahead"), move(far_high, back, "high_back")
        high, far_low = move(high, ahead, "high_ahead"), move(far_low, back, "low_back")
        behind.append((low, high))
        beyond.append((far_low, far_high))

    advance()
    col = lax.axis_index("col")
    stored, stored_index = b_values[:, 0], b_index.reshape(-1)
    other = lax.ppermute(stored, "col", swap)
    other_index = lax.ppermute(stored_index, "col", swap)
    inner_width = 2 * stored.shape[0] // n
    right = densify(col[None], stored_index, other_index, stored, other, n // 2, inner_width)

    around = np.array([[order[(order.index(r) + o) % n] for o in range(n)] for r in range(n)])
    cycle = lax.dynamic_index_in_dim(
        jnp.asarray(around, jnp.int32), lax.axis_index("row"), 0, keepdims=False
    )

    def after(done):
        low, far_high, done = lax.optimization_barrier((behind[-1][0], beyond[-1][1], done))
        behind[-1] = (low, behind[-1][1])
        beyond[-1] = (beyond[-1][0], far_high)
        return done


    right = after(right)
    total = None
    for k in range(1, whole_steps + 1):
        offsets, items = (n - k, k), [behind[k], beyond[k]]
        if k == 1:
            offsets, items = (0, *offsets), [behind[0], *items]
        if k < whole_steps:
            advance()
        else:
            small = half // 4
            at = small * slots * blk
            low, high = behind[-1][0], beyond[-1][1]
            large_parts = (
                small,
                half - small,
                move(low[at:], ahead, "far_low_ahead"),
                move(high[at:], back, "far_high_back"),
            )
        index = [read_note(behind[k][0]), read_note(beyond[k][1])]
        if k == 1:
            index.insert(0, own_index)
        total = product(cycle, offsets, index, items, right, total, (0, half), half, rows)
        if k < whole_steps:
            total = after(total)
    low, high = behind[-1][0][:at], beyond[-1][1][:at]
    small_parts = (0, small, move(low, ahead, "last_low_ahead"), move(high, back, "last_high_back"))
    last_parts = [large_parts, small_parts]
    out = None
    far_index = read_note(last_parts[0][2])
    for start, size, low, high in last_parts:
        starts = (start, half + start)
        out = finish(
            cycle, n // 2, far_index, low, high, right, total, starts, size, out
        )
    return out


def solution(mesh):
    placed = (
        P(("groups", "col"), "row", None, None, None),
        P(("groups", "col"), "row", None),
        P(("groups", "col"), "row", None, None, None),
        P(("groups", "col"), "row", None),
    )
    return jax.shard_map(
        body,
        mesh=mesh,
        in_specs=placed,
        out_specs=P(("groups", "col"), "row", None, None, None),
        check_vma=False,
    )
```

```python
import functools

import jax
import jax.numpy as jnp
import numpy as np
from jax import lax
from jax.experimental import pallas as pl
from jax.experimental.pallas import tpu as pltpu
from jax.sharding import PartitionSpec as P

BJ = 8
NOTE_ROWS = 16
VMEM_LIMIT = 20 * 1024 * 1024


def ring_order(n):
    if n == 8:
        return (0, 2, 4, 6, 7, 5, 3, 1)
    return tuple(range(n))


def densify_kernel(col_ref, own_index, other_index, own_ref, other_ref, dense_ref):
    source = pl.program_id(0)
    first = pl.program_id(1) * own_ref.shape[0]
    blk = own_ref.shape[-1]
    slots = own_ref.shape[1]
    for k in range(own_ref.shape[0]):
        stored = [
            jnp.where(source == 0, own_ref[k, t], other_ref[k, t]).astype(jnp.float32)
            for t in range(slots)
        ]
        at = [(first + k) * slots + t for t in range(slots)]
        columns = [jnp.where(source == 0, own_index[i], other_index[i]) for i in at]
        for j in range(BJ):
            total = jnp.zeros((blk, blk), jnp.float32)
            for t in range(slots):
                total = total + jnp.where(columns[t] == j, stored[t], 0.0)
            dense_ref[0, k, :, j * blk : (j + 1) * blk] = total.astype(jnp.bfloat16)


def densify(col, own_index, other_index, own, other, pieces, inner_width):
    slots, blk = own.shape[1], own.shape[-1]
    stored = (inner_width, slots, blk, blk)
    return pl.pallas_call(
        densify_kernel,
        out_shape=jax.ShapeDtypeStruct((2 * pieces, inner_width, blk, BJ * blk), jnp.bfloat16),
        grid_spec=pltpu.PrefetchScalarGridSpec(
            num_scalar_prefetch=3,
            grid=(2, pieces),
            in_specs=[
                pl.BlockSpec(stored, lambda s, g, c, *i: (jnp.where(s == 0, g, pieces - 1), 0, 0, 0)),
                pl.BlockSpec(stored, lambda s, g, c, *i: (jnp.where(s == 0, 0, g), 0, 0, 0)),
            ],
            out_specs=pl.BlockSpec(
                (1, inner_width, blk, BJ * blk),
                lambda s, g, c, *i: (jnp.where(s == 0, c[0], 1 - c[0]) * pieces + g, 0, 0, 0),
            ),
        ),
        compiler_params=pltpu.CompilerParams(vmem_limit_bytes=VMEM_LIMIT),
        name="densify",
        cost_estimate=pl.CostEstimate(flops=0, bytes_accessed=0, transcendentals=0),
    )(col, own_index, other_index, own, other)


def product_kernel(offsets, sides, starts, has_total, step, *refs):
    count = len(offsets)
    index = refs[1 : 1 + count]
    refs = refs[1 + count :]
    left = refs[: count * sides]
    right = refs[count * sides : count * (sides + 1)]
    rest = refs[count * (sides + 1) :]
    out_ref, held = (rest[-2], rest[-1]) if sides == 2 else (rest[-1], None)
    total_ref = rest[0] if has_total else None
    slots, blk = index[0].shape[0], left[0].shape[-1]
    wide = 2 * blk
    g = pl.program_id(0)
    if sides == 2:
        each = pl.num_programs(0) // 2
        second = g >= each
        row0 = jnp.where(second, starts[1] + (g - each) * step, starts[0] + g * step)
    else:
        row0 = starts[0] + g * step
    if sides == 2:
        for m in range(count):

            @pl.when(g < each)
            def _(m=m):
                held[m] = left[m * 2][...]

            @pl.when(g >= each)
            def _(m=m):
                held[m] = left[m * 2 + 1][...]

    for i in range(step):
        factors = []
        for m in range(count):
            inner = [index[m][s, row0 + i] for s in range(slots)]
            parts = []
            for s in range(slots):
                at = slice((i * slots + s) * blk, (i * slots + s + 1) * blk)
                part = left[m][at, :] if sides == 1 else held[m, at, :]
                parts.append(part * jnp.where(inner[s] >= 0, 1.0, 0.0).astype(jnp.bfloat16))
            factors.append((jnp.concatenate(parts, axis=1), [jnp.maximum(k, 0) for k in inner]))
        for c in range(BJ // 2):
            columns = slice(c * wide, (c + 1) * wide)
            total = total_ref[i, :, columns] if has_total else None
            for m in range(count):
                row, inner = factors[m]
                rows_of = jnp.concatenate([right[m][0, k, :, columns] for k in inner], axis=0)
                term = jnp.dot(row, rows_of, preferred_element_type=jnp.float32)
                total = term if total is None else total + term
            out_ref[i, :, columns] = total


def product(cycle, offsets, index, left, right, total, starts, size, rows, step=4):
    count, sides = len(offsets), len(starts)
    slots, blk = index[0].shape[0], left[0][0].shape[-1]
    each = size // step
    inner_width = right.shape[1]

    def of_side(s):
        if s == 0:
            return lambda g, *p: (jnp.minimum(g, each - 1), 0)
        return lambda g, *p: (jnp.maximum(g - each, 0), 0)

    def place(g):
        if sides == 1:
            return starts[0] // step + g
        return jnp.where(g < each, starts[0] // step + g, starts[1] // step + g - each)

    in_specs = [
        pl.BlockSpec((step * slots * blk, blk), of_side(s)) for _ in range(count) for s in range(sides)
    ]
    in_specs += [
        pl.BlockSpec(
            (1, inner_width, blk, BJ * blk), functools.partial(lambda o, g, c, *p: (c[o], 0, 0, 0), o)
        )
        for o in offsets
    ]
    operands = [cycle, *index, *(array for piece in left for array in piece), *([right] * count)]
    aliases = {}
    if total is not None:
        in_specs.append(pl.BlockSpec((step, blk, BJ * blk), lambda g, *p: (place(g), 0, 0)))
        operands.append(total)
        aliases = {len(operands) - 1: 0}
    out_shape = jax.ShapeDtypeStruct((rows, blk, BJ * blk), jnp.float32)
    out_spec = pl.BlockSpec((step, blk, BJ * blk), lambda g, *p: (place(g), 0, 0))
    return pl.pallas_call(
        functools.partial(
            product_kernel, offsets, sides, starts, total is not None, step
        ),
        out_shape=out_shape,
        grid_spec=pltpu.PrefetchScalarGridSpec(
            num_scalar_prefetch=1 + count,
            grid=(each * sides,),
            in_specs=in_specs,
            out_specs=out_spec,
            scratch_shapes=[pltpu.VMEM((count, step * slots * blk, blk), jnp.bfloat16)] * (sides - 1),
        ),
        input_output_aliases=aliases,
        compiler_params=pltpu.CompilerParams(vmem_limit_bytes=VMEM_LIMIT),
        name="product",
        cost_estimate=pl.CostEstimate(flops=0, bytes_accessed=0, transcendentals=0),
    )(*operands)


def finish_kernel(offset, starts, size, cycle, index, low, high, right, total, *refs):
    out_ref, staged, sems = refs[-3:]
    slots, blk = index.shape[0], low.shape[-1]
    wide = 2 * blk
    copies = []
    for half_ref, start in ((low, starts[0]), (high, starts[1])):
        for i in range(size):
            row, at = start + i, len(copies)
            inner = [index[s, row] for s in range(slots)]
            parts = []
            for s in range(slots):
                part = half_ref[(i * slots + s) * blk : (i * slots + s + 1) * blk, :]
                parts.append(part * jnp.where(inner[s] >= 0, 1.0, 0.0).astype(jnp.bfloat16))
            factor = jnp.concatenate(parts, axis=1)
            for c in range(BJ // 2):
                columns = slice(c * wide, (c + 1) * wide)
                rows_of = jnp.concatenate(
                    [right[0, jnp.maximum(k, 0), :, columns] for k in inner], axis=0
                )
                term = jnp.dot(factor, rows_of, preferred_element_type=jnp.float32)
                result = (total[row, :, columns] + term).astype(jnp.bfloat16)
                for j in range(2):
                    staged[at, c * 2 + j] = result[:, j * blk : (j + 1) * blk]
            copies.append(pltpu.make_async_copy(staged.at[at], out_ref.at[row, 0], sems.at[at]))
            copies[-1].start()
    for copy in copies:
        copy.wait()


def finish(cycle, offset, index, low, high, right, total, starts, size, target):
    rows, blk = total.shape[0], total.shape[1]
    inner_width = right.shape[1]
    whole = pl.BlockSpec(memory_space=pltpu.VMEM)
    piece = pl.BlockSpec(
        (1, inner_width, blk, BJ * blk), lambda g, c, *p: (c[offset], 0, 0, 0)
    )
    operands = [cycle, index, low, high, right, total]
    in_specs = [whole, whole, piece, whole]
    aliases = {}
    if target is not None:
        in_specs.append(pl.BlockSpec(memory_space=pl.ANY))
        operands.append(target)
        aliases = {len(operands) - 1: 0}
    return pl.pallas_call(
        functools.partial(finish_kernel, offset, starts, size),
        out_shape=jax.ShapeDtypeStruct((rows, 1, BJ, blk, blk), jnp.bfloat16),
        grid_spec=pltpu.PrefetchScalarGridSpec(
            num_scalar_prefetch=2,
            grid=(1,),
            in_specs=in_specs,
            out_specs=pl.BlockSpec(memory_space=pl.ANY),
            scratch_shapes=[
                pltpu.VMEM((2 * size, BJ, blk, blk), jnp.bfloat16),
                pltpu.SemaphoreType.DMA((2 * size,)),
            ],
        ),
        input_output_aliases=aliases,
        compiler_params=pltpu.CompilerParams(vmem_limit_bytes=VMEM_LIMIT),
        name="finish",
        cost_estimate=pl.CostEstimate(flops=0, bytes_accessed=0, transcendentals=0),
    )(*operands)


def pack_kernel(flat_ref, index_hbm, low_ref, high_ref, index_ref, wide_ref, sems):
    cut = flat_ref.shape[0] // 2
    index_copy = pltpu.make_async_copy(index_hbm, index_ref, sems.at[2])
    index_copy.start()
    copies = [
        pltpu.make_async_copy(
            flat_ref.at[pl.ds(h * cut, cut)], half_ref.at[pl.ds(0, cut)], sems.at[h]
        )
        for h, half_ref in enumerate((low_ref, high_ref))
    ]
    for copy in copies:
        copy.start()
    index_copy.wait()
    wide_ref[...] = jnp.zeros(wide_ref.shape, jnp.float32)
    wide_ref[: index_ref.shape[0], : index_ref.shape[1]] = index_ref[...].astype(jnp.float32)
    note = wide_ref[...].astype(jnp.bfloat16)
    for half_ref in (low_ref, high_ref):
        half_ref[cut:] = note
    for copy in copies:
        copy.wait()


def pack(flat, index):
    size, blk = flat.shape
    half = jax.ShapeDtypeStruct((size // 2 + NOTE_ROWS, blk), jnp.bfloat16)
    return pl.pallas_call(
        pack_kernel,
        out_shape=(half, half),
        in_specs=[pl.BlockSpec(memory_space=pl.ANY)] * 2,
        out_specs=[pl.BlockSpec(memory_space=pltpu.VMEM)] * 2,
        scratch_shapes=[
            pltpu.VMEM(index.shape, jnp.int32),
            pltpu.VMEM((NOTE_ROWS, blk), jnp.float32),
            pltpu.SemaphoreType.DMA((3,)),
        ],
        compiler_params=pltpu.CompilerParams(vmem_limit_bytes=VMEM_LIMIT),
        name="pack",
        cost_estimate=pl.CostEstimate(flops=0, bytes_accessed=0, transcendentals=0),
    )(*(pltpu.with_memory_space_constraint(x, pltpu.HBM) for x in (flat, index)))


def body(a_values, a_index, b_values, b_index):
    n = lax.axis_size("row")
    order = ring_order(n)
    ahead = [(order[q], order[(q + 1) % n]) for q in range(n)]
    back = [(dst, src) for src, dst in ahead]
    whole_steps = n // 2 - 1
    rows, _, slots, blk, _ = a_values.shape
    half = rows // 2

    swap = [(0, 1), (1, 0)]
    flat = a_values.reshape(rows * slots * blk, blk)
    cut = half * slots * blk
    own_index = a_index[:, 0].T
    low_first, high_first = pack(flat, own_index)
    low_second, high_second = flat[:cut], flat[cut:]

    def read_note(message):
        return message[-NOTE_ROWS:][:slots, :rows].astype(jnp.int32)

    def move(array, way, name):
        with jax.named_scope(name):
            return lax.ppermute(array, "row", way)

    behind, beyond = [(low_first, high_second)], [(low_second, high_first)]

    def advance():
        low, high = behind[-1]
        far_low, far_high = beyond[-1]
        low, far_high = move(low, ahead, "low_ahead"), move(far_high, back, "high_back")
        high, far_low = move(high, ahead, "high_ahead"), move(far_low, back, "low_back")
        behind.append((low, high))
        beyond.append((far_low, far_high))

    advance()
    col = lax.axis_index("col")
    stored = b_values[:, 0]
    other, stored_index = lax.optimization_barrier((lax.ppermute(stored, "col", swap), b_index))
    stored_index = stored_index.reshape(-1)
    other_index = lax.ppermute(stored_index, "col", swap)
    inner_width = 2 * stored.shape[0] // n
    right = densify(col[None], stored_index, other_index, stored, other, n // 2, inner_width)

    around = np.array([[order[(order.index(r) + o) % n] for o in range(n)] for r in range(n)])
    cycle = lax.dynamic_index_in_dim(
        jnp.asarray(around, jnp.int32), lax.axis_index("row"), 0, keepdims=False
    )

    def after(done):
        low, far_high, done = lax.optimization_barrier((behind[-1][0], beyond[-1][1], done))
        behind[-1] = (low, behind[-1][1])
        beyond[-1] = (beyond[-1][0], far_high)
        return done


    total = None
    for k in range(1, whole_steps + 1):
        offsets, items = (n - k, k), [behind[k], beyond[k]]
        if k == 1:
            offsets, items = (0, *offsets), [behind[0], *items]
        if k < whole_steps:
            advance()
        else:
            small = half // 4
            at = small * slots * blk
            low, high = behind[-1][0], beyond[-1][1]
            large_parts = (
                small,
                half - small,
                move(low[at:], ahead, "far_low_ahead"),
                move(high[at:], back, "far_high_back"),
            )
        index = [read_note(behind[k][0]), read_note(beyond[k][1])]
        if k == 1:
            index.insert(0, own_index)
        total = product(cycle, offsets, index, items, right, total, (0, half), half, rows)
        if k < whole_steps:
            total = after(total)
    low, high = behind[-1][0][:at], beyond[-1][1][:at]
    small_parts = (0, small, move(low, ahead, "last_low_ahead"), move(high, back, "last_high_back"))
    last_parts = [large_parts, small_parts]
    out = None
    far_index = read_note(last_parts[0][2])
    for start, size, low, high in last_parts:
        starts = (start, half + start)
        out = finish(
            cycle, n // 2, far_index, low, high, right, total, starts, size, out
        )
    return out


def solution(mesh):
    placed = (
        P(("groups", "col"), "row", None, None, None),
        P(("groups", "col"), "row", None),
        P(("groups", "col"), "row", None, None, None),
        P(("groups", "col"), "row", None),
    )
    return jax.shard_map(
        body,
        mesh=mesh,
        in_specs=placed,
        out_specs=P(("groups", "col"), "row", None, None, None),
        check_vma=False,
    )
```

```python
import functools

import jax
import jax.numpy as jnp
import numpy as np
from jax import lax
from jax.experimental import pallas as pl
from jax.experimental.pallas import tpu as pltpu
from jax.sharding import PartitionSpec as P

BJ = 8
NOTE_ROWS = 16
VMEM_LIMIT = 20 * 1024 * 1024


def ring_order(n):
    if n == 8:
        return (0, 2, 4, 6, 7, 5, 3, 1)
    return tuple(range(n))


def densify_kernel(col_ref, own_index, other_index, own_ref, other_ref, dense_ref):
    source = pl.program_id(0)
    first = pl.program_id(1) * own_ref.shape[0]
    blk = own_ref.shape[-1]
    slots = own_ref.shape[1]
    for k in range(own_ref.shape[0]):
        stored = [
            jnp.where(source == 0, own_ref[k, t], other_ref[k, t]).astype(jnp.float32)
            for t in range(slots)
        ]
        at = [(first + k) * slots + t for t in range(slots)]
        columns = [jnp.where(source == 0, own_index[i], other_index[i]) for i in at]
        for j in range(BJ):
            total = jnp.zeros((blk, blk), jnp.float32)
            for t in range(slots):
                total = total + jnp.where(columns[t] == j, stored[t], 0.0)
            dense_ref[0, k, :, j * blk : (j + 1) * blk] = total.astype(jnp.bfloat16)


def densify(col, own_index, other_index, own, other, pieces, inner_width):
    slots, blk = own.shape[1], own.shape[-1]
    stored = (inner_width, slots, blk, blk)
    return pl.pallas_call(
        densify_kernel,
        out_shape=jax.ShapeDtypeStruct((2 * pieces, inner_width, blk, BJ * blk), jnp.bfloat16),
        grid_spec=pltpu.PrefetchScalarGridSpec(
            num_scalar_prefetch=3,
            grid=(2, pieces),
            in_specs=[
                pl.BlockSpec(stored, lambda s, g, c, *i: (jnp.where(s == 0, g, pieces - 1), 0, 0, 0)),
                pl.BlockSpec(stored, lambda s, g, c, *i: (jnp.where(s == 0, 0, g), 0, 0, 0)),
            ],
            out_specs=pl.BlockSpec(
                (1, inner_width, blk, BJ * blk),
                lambda s, g, c, *i: (jnp.where(s == 0, c[0], 1 - c[0]) * pieces + g, 0, 0, 0),
            ),
        ),
        compiler_params=pltpu.CompilerParams(vmem_limit_bytes=VMEM_LIMIT),
        name="densify",
        cost_estimate=pl.CostEstimate(flops=0, bytes_accessed=0, transcendentals=0),
    )(col, own_index, other_index, own, other)


def product_kernel(offsets, sides, starts, has_total, step, *refs):
    count = len(offsets)
    index = refs[1 : 1 + count]
    refs = refs[1 + count :]
    left = refs[: count * sides]
    right = refs[count * sides : count * (sides + 1)]
    rest = refs[count * (sides + 1) :]
    out_ref, held = (rest[-2], rest[-1]) if sides == 2 else (rest[-1], None)
    total_ref = rest[0] if has_total else None
    slots, blk = index[0].shape[0], left[0].shape[-1]
    wide = 2 * blk
    g = pl.program_id(0)
    if sides == 2:
        each = pl.num_programs(0) // 2
        second = g >= each
        row0 = jnp.where(second, starts[1] + (g - each) * step, starts[0] + g * step)
    else:
        row0 = starts[0] + g * step
    if sides == 2:
        for m in range(count):

            @pl.when(g < each)
            def _(m=m):
                held[m] = left[m * 2][...]

            @pl.when(g >= each)
            def _(m=m):
                held[m] = left[m * 2 + 1][...]

    for i in range(step):
        factors = []
        for m in range(count):
            inner = [index[m][s, row0 + i] for s in range(slots)]
            parts = []
            for s in range(slots):
                at = slice((i * slots + s) * blk, (i * slots + s + 1) * blk)
                part = left[m][at, :] if sides == 1 else held[m, at, :]
                parts.append(part * jnp.where(inner[s] >= 0, 1.0, 0.0).astype(jnp.bfloat16))
            factors.append((jnp.concatenate(parts, axis=1), [jnp.maximum(k, 0) for k in inner]))
        for c in range(BJ // 2):
            columns = slice(c * wide, (c + 1) * wide)
            total = total_ref[i, :, columns] if has_total else None
            for m in range(count):
                row, inner = factors[m]
                rows_of = jnp.concatenate([right[m][0, k, :, columns] for k in inner], axis=0)
                term = jnp.dot(row, rows_of, preferred_element_type=jnp.float32)
                total = term if total is None else total + term
            out_ref[i, :, columns] = total


def product(cycle, offsets, index, left, right, total, starts, size, rows, step=4):
    count, sides = len(offsets), len(starts)
    slots, blk = index[0].shape[0], left[0][0].shape[-1]
    each = size // step
    inner_width = right.shape[1]

    def of_side(s):
        if s == 0:
            return lambda g, *p: (jnp.minimum(g, each - 1), 0)
        return lambda g, *p: (jnp.maximum(g - each, 0), 0)

    def place(g):
        if sides == 1:
            return starts[0] // step + g
        return jnp.where(g < each, starts[0] // step + g, starts[1] // step + g - each)

    in_specs = [
        pl.BlockSpec((step * slots * blk, blk), of_side(s)) for _ in range(count) for s in range(sides)
    ]
    in_specs += [
        pl.BlockSpec(
            (1, inner_width, blk, BJ * blk), functools.partial(lambda o, g, c, *p: (c[o], 0, 0, 0), o)
        )
        for o in offsets
    ]
    operands = [cycle, *index, *(array for piece in left for array in piece), *([right] * count)]
    aliases = {}
    if total is not None:
        in_specs.append(pl.BlockSpec((step, blk, BJ * blk), lambda g, *p: (place(g), 0, 0)))
        operands.append(total)
        aliases = {len(operands) - 1: 0}
    out_shape = jax.ShapeDtypeStruct((rows, blk, BJ * blk), jnp.float32)
    out_spec = pl.BlockSpec((step, blk, BJ * blk), lambda g, *p: (place(g), 0, 0))
    return pl.pallas_call(
        functools.partial(
            product_kernel, offsets, sides, starts, total is not None, step
        ),
        out_shape=out_shape,
        grid_spec=pltpu.PrefetchScalarGridSpec(
            num_scalar_prefetch=1 + count,
            grid=(each * sides,),
            in_specs=in_specs,
            out_specs=out_spec,
            scratch_shapes=[pltpu.VMEM((count, step * slots * blk, blk), jnp.bfloat16)] * (sides - 1),
        ),
        input_output_aliases=aliases,
        compiler_params=pltpu.CompilerParams(vmem_limit_bytes=VMEM_LIMIT),
        name="product",
        cost_estimate=pl.CostEstimate(flops=0, bytes_accessed=0, transcendentals=0),
    )(*operands)


def finish_kernel(parts, offset, cycle_ref, index_ref, right, total, *refs):
    out_ref, staged, sems = refs[-3:]
    arrays = refs[: len(refs) - 3]
    slots, blk = index_ref.shape[0], right.shape[2]
    wide = 2 * blk
    index, piece = index_ref[...], cycle_ref[...][0, offset]
    copies = []
    for at, (row, places) in enumerate(parts):
        inner = [index[s, row] for s in range(slots)]
        factor = []
        for s, (array, start) in enumerate(places):
            filled = jnp.where(inner[s] >= 0, 1.0, 0.0).astype(jnp.bfloat16)
            factor.append(arrays[array][start : start + blk, :] * filled)
        factor = jnp.concatenate(factor, axis=1)
        for c in range(BJ // 2):
            columns = slice(c * wide, (c + 1) * wide)
            rows_of = jnp.concatenate(
                [right[piece, jnp.maximum(k, 0), :, columns] for k in inner], axis=0
            )
            term = jnp.dot(factor, rows_of, preferred_element_type=jnp.float32)
            result = (total[row, :, columns] + term).astype(jnp.bfloat16)
            for j in range(2):
                staged[at, c * 2 + j] = result[:, j * blk : (j + 1) * blk]
        copies.append(pltpu.make_async_copy(staged.at[at], out_ref.at[row, 0], sems.at[at]))
        copies[-1].start()
    for copy in copies:
        copy.wait()


def finish(parts, cycle, offset, index, right, total, arrays, target):
    rows, blk = total.shape[0], total.shape[1]
    whole = pl.BlockSpec(memory_space=pltpu.VMEM)
    operands = [cycle[None], index, right, total, *arrays]
    in_specs = [whole] * len(operands)
    aliases = {}
    if target is not None:
        in_specs.append(pl.BlockSpec(memory_space=pl.ANY))
        operands.append(target)
        aliases = {len(operands) - 1: 0}
    return pl.pallas_call(
        functools.partial(finish_kernel, parts, offset),
        out_shape=jax.ShapeDtypeStruct((rows, 1, BJ, blk, blk), jnp.bfloat16),
        in_specs=in_specs,
        out_specs=pl.BlockSpec(memory_space=pl.ANY),
        scratch_shapes=[
            pltpu.VMEM((len(parts), BJ, blk, blk), jnp.bfloat16),
            pltpu.SemaphoreType.DMA((len(parts),)),
        ],
        input_output_aliases=aliases,
        compiler_params=pltpu.CompilerParams(vmem_limit_bytes=VMEM_LIMIT // 2),
        name="finish",
        cost_estimate=pl.CostEstimate(flops=0, bytes_accessed=0, transcendentals=0),
    )(*operands)


def pack_kernel(flat_ref, index_hbm, low_ref, high_ref, index_ref, wide_ref, sems):
    cut = flat_ref.shape[0] // 2
    index_copy = pltpu.make_async_copy(index_hbm, index_ref, sems.at[2])
    index_copy.start()
    copies = [
        pltpu.make_async_copy(
            flat_ref.at[pl.ds(h * cut, cut)], half_ref.at[pl.ds(0, cut)], sems.at[h]
        )
        for h, half_ref in enumerate((low_ref, high_ref))
    ]
    for copy in copies:
        copy.start()
    index_copy.wait()
    wide_ref[...] = jnp.zeros(wide_ref.shape, jnp.float32)
    wide_ref[: index_ref.shape[0], : index_ref.shape[1]] = index_ref[...].astype(jnp.float32)
    note = wide_ref[...].astype(jnp.bfloat16)
    for half_ref in (low_ref, high_ref):
        half_ref[cut:] = note
    for copy in copies:
        copy.wait()


def pack(flat, index):
    size, blk = flat.shape
    half = jax.ShapeDtypeStruct((size // 2 + NOTE_ROWS, blk), jnp.bfloat16)
    return pl.pallas_call(
        pack_kernel,
        out_shape=(half, half),
        in_specs=[pl.BlockSpec(memory_space=pl.ANY)] * 2,
        out_specs=[pl.BlockSpec(memory_space=pltpu.VMEM)] * 2,
        scratch_shapes=[
            pltpu.VMEM(index.shape, jnp.int32),
            pltpu.VMEM((NOTE_ROWS, blk), jnp.float32),
            pltpu.SemaphoreType.DMA((3,)),
        ],
        compiler_params=pltpu.CompilerParams(vmem_limit_bytes=VMEM_LIMIT),
        name="pack",
        cost_estimate=pl.CostEstimate(flops=0, bytes_accessed=0, transcendentals=0),
    )(*(pltpu.with_memory_space_constraint(x, pltpu.HBM) for x in (flat, index)))


def body(a_values, a_index, b_values, b_index):
    n = lax.axis_size("row")
    order = ring_order(n)
    ahead = [(order[q], order[(q + 1) % n]) for q in range(n)]
    back = [(dst, src) for src, dst in ahead]
    whole_steps = n // 2 - 1
    rows, _, slots, blk, _ = a_values.shape
    half = rows // 2

    swap = [(0, 1), (1, 0)]
    flat = a_values.reshape(rows * slots * blk, blk)
    cut = half * slots * blk
    own_index = a_index[:, 0].T
    low_first, high_first = pack(flat, own_index)
    low_second, high_second = flat[:cut], flat[cut:]

    def read_note(message):
        return message[-NOTE_ROWS:][:slots, :rows].astype(jnp.int32)

    def move(array, way, name):
        with jax.named_scope(name):
            return lax.ppermute(array, "row", way)

    behind, beyond = [(low_first, high_second)], [(low_second, high_first)]

    def advance():
        low, high = behind[-1]
        far_low, far_high = beyond[-1]
        low, far_high = move(low, ahead, "low_ahead"), move(far_high, back, "high_back")
        high, far_low = move(high, ahead, "high_ahead"), move(far_low, back, "low_back")
        behind.append((low, high))
        beyond.append((far_low, far_high))

    advance()
    col = lax.axis_index("col")
    stored = b_values[:, 0]
    other, stored_index = lax.optimization_barrier((lax.ppermute(stored, "col", swap), b_index))
    stored_index = stored_index.reshape(-1)
    other_index = lax.ppermute(stored_index, "col", swap)
    inner_width = 2 * stored.shape[0] // n
    right = densify(col[None], stored_index, other_index, stored, other, n // 2, inner_width)

    around = np.array([[order[(order.index(r) + o) % n] for o in range(n)] for r in range(n)])
    cycle = lax.dynamic_index_in_dim(
        jnp.asarray(around, jnp.int32), lax.axis_index("row"), 0, keepdims=False
    )

    def after(done):
        low, far_high, done = lax.optimization_barrier((behind[-1][0], beyond[-1][1], done))
        behind[-1] = (low, behind[-1][1])
        beyond[-1] = (beyond[-1][0], far_high)
        return done


    total = None
    for k in range(1, whole_steps + 1):
        offsets, items = (n - k, k), [behind[k], beyond[k]]
        if k == 1:
            offsets, items = (0, *offsets), [behind[0], *items]
        if k < whole_steps:
            advance()
        else:
            small = half // 4
            at = small * slots * blk
            low, high = behind[-1][0], beyond[-1][1]
            large_parts = (
                small,
                half - small,
                move(low[at:], ahead, "far_low_ahead"),
                move(high[at:], back, "far_high_back"),
            )
        index = [read_note(behind[k][0]), read_note(beyond[k][1])]
        if k == 1:
            index.insert(0, own_index)
        total = product(cycle, offsets, index, items, right, total, (0, half), half, rows)
        if k < whole_steps:
            total = after(total)
    low, high = behind[-1][0][:at], beyond[-1][1][:at]
    small_parts = (0, small, move(low, ahead, "last_low_ahead"), move(high, back, "last_high_back"))
    last_parts = [large_parts, small_parts]
    out = None
    far_index = read_note(last_parts[0][2])
    per_row = slots * blk
    for start, size, low, high in last_parts:
        parts = [
            (h * half + start + i, [(h, i * per_row + s * blk) for s in range(slots)])
            for h in range(2)
            for i in range(size)
        ]
        out = finish(parts, cycle, n // 2, far_index, right, total, [low, high], out)
    return out


def solution(mesh):
    placed = (
        P(("groups", "col"), "row", None, None, None),
        P(("groups", "col"), "row", None),
        P(("groups", "col"), "row", None, None, None),
        P(("groups", "col"), "row", None),
    )
    return jax.shard_map(
        body,
        mesh=mesh,
        in_specs=placed,
        out_specs=P(("groups", "col"), "row", None, None, None),
        check_vma=False,
    )
```

```python
import functools

import jax
import jax.numpy as jnp
import numpy as np
from jax import lax
from jax.experimental import pallas as pl
from jax.experimental.pallas import tpu as pltpu
from jax.sharding import PartitionSpec as P

BJ = 8
NOTE_ROWS = 16
VMEM_LIMIT = 20 * 1024 * 1024


def ring_order(n):
    if n == 8:
        return (0, 2, 4, 6, 7, 5, 3, 1)
    return tuple(range(n))


def densify_kernel(col_ref, own_index, other_index, own_ref, other_ref, dense_ref):
    source = pl.program_id(0)
    first = pl.program_id(1) * own_ref.shape[0]
    blk = own_ref.shape[-1]
    slots = own_ref.shape[1]
    for k in range(own_ref.shape[0]):
        stored = [
            jnp.where(source == 0, own_ref[k, t], other_ref[k, t]).astype(jnp.float32)
            for t in range(slots)
        ]
        at = [(first + k) * slots + t for t in range(slots)]
        columns = [jnp.where(source == 0, own_index[i], other_index[i]) for i in at]
        for j in range(BJ):
            total = jnp.zeros((blk, blk), jnp.float32)
            for t in range(slots):
                total = total + jnp.where(columns[t] == j, stored[t], 0.0)
            dense_ref[0, k, :, j * blk : (j + 1) * blk] = total.astype(jnp.bfloat16)


def densify(col, own_index, other_index, own, other, pieces, inner_width):
    slots, blk = own.shape[1], own.shape[-1]
    stored = (inner_width, slots, blk, blk)
    return pl.pallas_call(
        densify_kernel,
        out_shape=jax.ShapeDtypeStruct((2 * pieces, inner_width, blk, BJ * blk), jnp.bfloat16),
        grid_spec=pltpu.PrefetchScalarGridSpec(
            num_scalar_prefetch=3,
            grid=(2, pieces),
            in_specs=[
                pl.BlockSpec(stored, lambda s, g, c, *i: (jnp.where(s == 0, g, pieces - 1), 0, 0, 0)),
                pl.BlockSpec(stored, lambda s, g, c, *i: (jnp.where(s == 0, 0, g), 0, 0, 0)),
            ],
            out_specs=pl.BlockSpec(
                (1, inner_width, blk, BJ * blk),
                lambda s, g, c, *i: (jnp.where(s == 0, c[0], 1 - c[0]) * pieces + g, 0, 0, 0),
            ),
        ),
        compiler_params=pltpu.CompilerParams(vmem_limit_bytes=VMEM_LIMIT),
        name="densify",
        cost_estimate=pl.CostEstimate(flops=0, bytes_accessed=0, transcendentals=0),
    )(col, own_index, other_index, own, other)


def product_kernel(offsets, sides, starts, has_total, step, *refs):
    count = len(offsets)
    index = refs[1 : 1 + count]
    refs = refs[1 + count :]
    left = refs[: count * sides]
    right = refs[count * sides : count * (sides + 1)]
    rest = refs[count * (sides + 1) :]
    out_ref, held = (rest[-2], rest[-1]) if sides == 2 else (rest[-1], None)
    total_ref = rest[0] if has_total else None
    slots, blk = index[0].shape[0], left[0].shape[-1]
    wide = 2 * blk
    g = pl.program_id(0)
    if sides == 2:
        each = pl.num_programs(0) // 2
        second = g >= each
        row0 = jnp.where(second, starts[1] + (g - each) * step, starts[0] + g * step)
    else:
        row0 = starts[0] + g * step
    if sides == 2:
        for m in range(count):

            @pl.when(g < each)
            def _(m=m):
                held[m] = left[m * 2][...]

            @pl.when(g >= each)
            def _(m=m):
                held[m] = left[m * 2 + 1][...]

    for i in range(step):
        factors = []
        for m in range(count):
            inner = [index[m][s, row0 + i] for s in range(slots)]
            parts = []
            for s in range(slots):
                at = slice((i * slots + s) * blk, (i * slots + s + 1) * blk)
                part = left[m][at, :] if sides == 1 else held[m, at, :]
                parts.append(part * jnp.where(inner[s] >= 0, 1.0, 0.0).astype(jnp.bfloat16))
            factors.append((jnp.concatenate(parts, axis=1), [jnp.maximum(k, 0) for k in inner]))
        for c in range(BJ // 2):
            columns = slice(c * wide, (c + 1) * wide)
            total = total_ref[i, :, columns] if has_total else None
            for m in range(count):
                row, inner = factors[m]
                rows_of = jnp.concatenate([right[m][0, k, :, columns] for k in inner], axis=0)
                term = jnp.dot(row, rows_of, preferred_element_type=jnp.float32)
                total = term if total is None else total + term
            out_ref[i, :, columns] = total


def product(cycle, offsets, index, left, right, total, starts, size, rows, step=4):
    count, sides = len(offsets), len(starts)
    slots, blk = index[0].shape[0], left[0][0].shape[-1]
    each = size // step
    inner_width = right.shape[1]

    def of_side(s):
        if s == 0:
            return lambda g, *p: (jnp.minimum(g, each - 1), 0)
        return lambda g, *p: (jnp.maximum(g - each, 0), 0)

    def place(g):
        if sides == 1:
            return starts[0] // step + g
        return jnp.where(g < each, starts[0] // step + g, starts[1] // step + g - each)

    in_specs = [
        pl.BlockSpec((step * slots * blk, blk), of_side(s)) for _ in range(count) for s in range(sides)
    ]
    in_specs += [
        pl.BlockSpec(
            (1, inner_width, blk, BJ * blk), functools.partial(lambda o, g, c, *p: (c[o], 0, 0, 0), o)
        )
        for o in offsets
    ]
    operands = [cycle, *index, *(array for piece in left for array in piece), *([right] * count)]
    aliases = {}
    if total is not None:
        in_specs.append(pl.BlockSpec((step, blk, BJ * blk), lambda g, *p: (place(g), 0, 0)))
        operands.append(total)
        aliases = {len(operands) - 1: 0}
    out_shape = jax.ShapeDtypeStruct((rows, blk, BJ * blk), jnp.float32)
    out_spec = pl.BlockSpec((step, blk, BJ * blk), lambda g, *p: (place(g), 0, 0))
    return pl.pallas_call(
        functools.partial(
            product_kernel, offsets, sides, starts, total is not None, step
        ),
        out_shape=out_shape,
        grid_spec=pltpu.PrefetchScalarGridSpec(
            num_scalar_prefetch=1 + count,
            grid=(each * sides,),
            in_specs=in_specs,
            out_specs=out_spec,
            scratch_shapes=[pltpu.VMEM((count, step * slots * blk, blk), jnp.bfloat16)] * (sides - 1),
        ),
        input_output_aliases=aliases,
        compiler_params=pltpu.CompilerParams(vmem_limit_bytes=VMEM_LIMIT),
        name="product",
        cost_estimate=pl.CostEstimate(flops=0, bytes_accessed=0, transcendentals=0),
    )(*operands)


def finish_kernel(parts, offset, cycle_ref, index_ref, right, total, *refs):
    out_ref, staged, sems = refs[-3:]
    arrays = refs[: len(refs) - 3]
    slots, blk = index_ref.shape[0], right.shape[2]
    wide = 2 * blk
    index, piece = index_ref[...], cycle_ref[...][0, offset]
    copies = []
    for at, (row, places) in enumerate(parts):
        inner = [index[s, row] for s in range(slots)]
        factor = []
        for s, (array, start) in enumerate(places):
            filled = jnp.where(inner[s] >= 0, 1.0, 0.0).astype(jnp.bfloat16)
            factor.append(arrays[array][start : start + blk, :] * filled)
        factor = jnp.concatenate(factor, axis=1)
        for c in range(BJ // 2):
            columns = slice(c * wide, (c + 1) * wide)
            rows_of = jnp.concatenate(
                [right[piece, jnp.maximum(k, 0), :, columns] for k in inner], axis=0
            )
            term = jnp.dot(factor, rows_of, preferred_element_type=jnp.float32)
            result = (total[row, :, columns] + term).astype(jnp.bfloat16)
            for j in range(2):
                staged[at, c * 2 + j] = result[:, j * blk : (j + 1) * blk]
        copies.append(pltpu.make_async_copy(staged.at[at], out_ref.at[row, 0], sems.at[at]))
        copies[-1].start()
    for copy in copies:
        copy.wait()


def finish(parts, cycle, offset, index, right, total, arrays, target):
    rows, blk = total.shape[0], total.shape[1]
    whole = pl.BlockSpec(memory_space=pltpu.VMEM)
    operands = [cycle[None], index, right, total, *arrays]
    in_specs = [whole] * len(operands)
    aliases = {}
    if target is not None:
        in_specs.append(pl.BlockSpec(memory_space=pl.ANY))
        operands.append(target)
        aliases = {len(operands) - 1: 0}
    return pl.pallas_call(
        functools.partial(finish_kernel, parts, offset),
        out_shape=jax.ShapeDtypeStruct((rows, 1, BJ, blk, blk), jnp.bfloat16),
        in_specs=in_specs,
        out_specs=pl.BlockSpec(memory_space=pl.ANY),
        scratch_shapes=[
            pltpu.VMEM((len(parts), BJ, blk, blk), jnp.bfloat16),
            pltpu.SemaphoreType.DMA((len(parts),)),
        ],
        input_output_aliases=aliases,
        compiler_params=pltpu.CompilerParams(vmem_limit_bytes=VMEM_LIMIT // 2),
        name="finish",
        cost_estimate=pl.CostEstimate(flops=0, bytes_accessed=0, transcendentals=0),
    )(*operands)


def pack_kernel(flat_ref, index_hbm, low_ref, high_ref, index_ref, wide_ref, sems):
    cut = flat_ref.shape[0] // 2
    index_copy = pltpu.make_async_copy(index_hbm, index_ref, sems.at[2])
    index_copy.start()
    copies = [
        pltpu.make_async_copy(
            flat_ref.at[pl.ds(h * cut, cut)], half_ref.at[pl.ds(0, cut)], sems.at[h]
        )
        for h, half_ref in enumerate((low_ref, high_ref))
    ]
    for copy in copies:
        copy.start()
    index_copy.wait()
    wide_ref[...] = jnp.zeros(wide_ref.shape, jnp.float32)
    wide_ref[: index_ref.shape[0], : index_ref.shape[1]] = index_ref[...].astype(jnp.float32)
    note = wide_ref[...].astype(jnp.bfloat16)
    for half_ref in (low_ref, high_ref):
        half_ref[cut:] = note
    for copy in copies:
        copy.wait()


def pack(flat, index):
    size, blk = flat.shape
    half = pltpu.VMEM((size // 2 + NOTE_ROWS, blk), jnp.bfloat16)
    return pl.pallas_call(
        pack_kernel,
        out_shape=(half, half),
        in_specs=[pl.BlockSpec(memory_space=pl.ANY)] * 2,
        out_specs=[pl.BlockSpec(memory_space=pltpu.VMEM)] * 2,
        scratch_shapes=[
            pltpu.VMEM(index.shape, jnp.int32),
            pltpu.VMEM((NOTE_ROWS, blk), jnp.float32),
            pltpu.SemaphoreType.DMA((3,)),
        ],
        compiler_params=pltpu.CompilerParams(vmem_limit_bytes=VMEM_LIMIT),
        name="pack",
        cost_estimate=pl.CostEstimate(flops=0, bytes_accessed=0, transcendentals=0),
    )(*(pltpu.with_memory_space_constraint(x, pltpu.HBM) for x in (flat, index)))


def body(a_values, a_index, b_values, b_index):
    n = lax.axis_size("row")
    order = ring_order(n)
    ahead = [(order[q], order[(q + 1) % n]) for q in range(n)]
    back = [(dst, src) for src, dst in ahead]
    whole_steps = n // 2 - 1
    rows, _, slots, blk, _ = a_values.shape
    half = rows // 2

    swap = [(0, 1), (1, 0)]
    flat = a_values.reshape(rows * slots * blk, blk)
    cut = half * slots * blk
    own_index = a_index[:, 0].T
    low_first, high_first = pack(flat, own_index)
    low_second, high_second = flat[:cut], flat[cut:]

    def read_note(message):
        return message[-NOTE_ROWS:][:slots, :rows].astype(jnp.int32)

    def move(array, way, name):
        with jax.named_scope(name):
            return lax.ppermute(array, "row", way)

    behind, beyond = [(low_first, high_second)], [(low_second, high_first)]

    def advance():
        low, high = behind[-1]
        far_low, far_high = beyond[-1]
        low, far_high = move(low, ahead, "low_ahead"), move(far_high, back, "high_back")
        high, far_low = move(high, ahead, "high_ahead"), move(far_low, back, "low_back")
        behind.append((low, high))
        beyond.append((far_low, far_high))

    advance()
    col = lax.axis_index("col")
    stored = b_values[:, 0]
    other, stored_index = lax.optimization_barrier((lax.ppermute(stored, "col", swap), b_index))
    stored_index = stored_index.reshape(-1)
    other_index = lax.ppermute(stored_index, "col", swap)
    inner_width = 2 * stored.shape[0] // n
    right = densify(col[None], stored_index, other_index, stored, other, n // 2, inner_width)

    around = np.array([[order[(order.index(r) + o) % n] for o in range(n)] for r in range(n)])
    cycle = lax.dynamic_index_in_dim(
        jnp.asarray(around, jnp.int32), lax.axis_index("row"), 0, keepdims=False
    )

    def after(done):
        low, far_high, done = lax.optimization_barrier((behind[-1][0], beyond[-1][1], done))
        behind[-1] = (low, behind[-1][1])
        beyond[-1] = (beyond[-1][0], far_high)
        return done


    total = None
    for k in range(1, whole_steps + 1):
        offsets, items = (n - k, k), [behind[k], beyond[k]]
        if k == 1:
            offsets, items = (0, *offsets), [(behind[0][0], beyond[0][1]), *items]
        if k < whole_steps:
            advance()
        else:
            small = half // 4
            at = small * slots * blk
            low, high = behind[-1][0], beyond[-1][1]
            large_parts = (
                small,
                half - small,
                move(low[at:], ahead, "far_low_ahead"),
                move(high[at:], back, "far_high_back"),
            )
        index = [read_note(behind[k][0]), read_note(beyond[k][1])]
        if k == 1:
            index.insert(0, own_index)
        total = product(cycle, offsets, index, items, right, total, (0, half), half, rows)
        if k < whole_steps:
            total = after(total)
    low, high = behind[-1][0][:at], beyond[-1][1][:at]
    small_parts = (0, small, move(low, ahead, "last_low_ahead"), move(high, back, "last_high_back"))
    last_parts = [large_parts, small_parts]
    out = None
    far_index = read_note(last_parts[0][2])
    per_row = slots * blk
    for start, size, low, high in last_parts:
        parts = [
            (h * half + start + i, [(h, i * per_row + s * blk) for s in range(slots)])
            for h in range(2)
            for i in range(size)
        ]
        out = finish(parts, cycle, n // 2, far_index, right, total, [low, high], out)
    return out


def solution(mesh):
    placed = (
        P(("groups", "col"), "row", None, None, None),
        P(("groups", "col"), "row", None),
        P(("groups", "col"), "row", None, None, None),
        P(("groups", "col"), "row", None),
    )
    return jax.shard_map(
        body,
        mesh=mesh,
        in_specs=placed,
        out_specs=P(("groups", "col"), "row", None, None, None),
        check_vma=False,
    )
```

```python
import functools

import jax
import jax.numpy as jnp
import numpy as np
from jax import lax
from jax.experimental import pallas as pl
from jax.experimental.pallas import tpu as pltpu
from jax.sharding import PartitionSpec as P

BJ = 8
NOTE_ROWS = 16
VMEM_LIMIT = 20 * 1024 * 1024


def ring_order(n):
    if n == 8:
        return (0, 2, 4, 6, 7, 5, 3, 1)
    return tuple(range(n))


def densify_kernel(col_ref, own_index, other_index, own_ref, other_ref, dense_ref):
    source = pl.program_id(0)
    first = pl.program_id(1) * own_ref.shape[0]
    blk = own_ref.shape[-1]
    slots = own_ref.shape[1]
    for k in range(own_ref.shape[0]):
        stored = [
            jnp.where(source == 0, own_ref[k, t], other_ref[k, t]).astype(jnp.float32)
            for t in range(slots)
        ]
        at = [(first + k) * slots + t for t in range(slots)]
        columns = [jnp.where(source == 0, own_index[i], other_index[i]) for i in at]
        for j in range(BJ):
            total = jnp.zeros((blk, blk), jnp.float32)
            for t in range(slots):
                total = total + jnp.where(columns[t] == j, stored[t], 0.0)
            dense_ref[0, k, :, j * blk : (j + 1) * blk] = total.astype(jnp.bfloat16)


def densify(col, own_index, other_index, own, other, pieces, inner_width):
    slots, blk = own.shape[1], own.shape[-1]
    stored = (inner_width, slots, blk, blk)
    return pl.pallas_call(
        densify_kernel,
        out_shape=jax.ShapeDtypeStruct((2 * pieces, inner_width, blk, BJ * blk), jnp.bfloat16),
        grid_spec=pltpu.PrefetchScalarGridSpec(
            num_scalar_prefetch=3,
            grid=(2, pieces),
            in_specs=[
                pl.BlockSpec(stored, lambda s, g, c, *i: (jnp.where(s == 0, g, pieces - 1), 0, 0, 0)),
                pl.BlockSpec(stored, lambda s, g, c, *i: (jnp.where(s == 0, 0, g), 0, 0, 0)),
            ],
            out_specs=pl.BlockSpec(
                (1, inner_width, blk, BJ * blk),
                lambda s, g, c, *i: (jnp.where(s == 0, c[0], 1 - c[0]) * pieces + g, 0, 0, 0),
            ),
        ),
        compiler_params=pltpu.CompilerParams(vmem_limit_bytes=VMEM_LIMIT),
        name="densify",
        cost_estimate=pl.CostEstimate(flops=0, bytes_accessed=0, transcendentals=0),
    )(col, own_index, other_index, own, other)


def product_kernel(offsets, sides, starts, has_total, step, *refs):
    count = len(offsets)
    index = refs[1 : 1 + count]
    refs = refs[1 + count :]
    left = refs[: count * sides]
    right = refs[count * sides : count * (sides + 1)]
    rest = refs[count * (sides + 1) :]
    out_ref, held = (rest[-2], rest[-1]) if sides == 2 else (rest[-1], None)
    total_ref = rest[0] if has_total else None
    slots, blk = index[0].shape[0], left[0].shape[-1]
    wide = 2 * blk
    g = pl.program_id(0)
    if sides == 2:
        each = pl.num_programs(0) // 2
        second = g >= each
        row0 = jnp.where(second, starts[1] + (g - each) * step, starts[0] + g * step)
    else:
        row0 = starts[0] + g * step
    if sides == 2:
        for m in range(count):

            @pl.when(g < each)
            def _(m=m):
                held[m] = left[m * 2][...]

            @pl.when(g >= each)
            def _(m=m):
                held[m] = left[m * 2 + 1][...]

    for i in range(step):
        factors = []
        for m in range(count):
            inner = [index[m][s, row0 + i] for s in range(slots)]
            parts = []
            for s in range(slots):
                at = slice((i * slots + s) * blk, (i * slots + s + 1) * blk)
                part = left[m][at, :] if sides == 1 else held[m, at, :]
                parts.append(part * jnp.where(inner[s] >= 0, 1.0, 0.0).astype(jnp.bfloat16))
            factors.append((jnp.concatenate(parts, axis=1), [jnp.maximum(k, 0) for k in inner]))
        for c in range(BJ // 2):
            columns = slice(c * wide, (c + 1) * wide)
            total = total_ref[i, :, columns] if has_total else None
            for m in range(count):
                row, inner = factors[m]
                rows_of = jnp.concatenate([right[m][0, k, :, columns] for k in inner], axis=0)
                term = jnp.dot(row, rows_of, preferred_element_type=jnp.float32)
                total = term if total is None else total + term
            out_ref[i, :, columns] = total


def product(cycle, offsets, index, left, right, total, starts, size, rows, step=4):
    count, sides = len(offsets), len(starts)
    slots, blk = index[0].shape[0], left[0][0].shape[-1]
    each = size // step
    inner_width = right.shape[1]

    def of_side(s):
        if s == 0:
            return lambda g, *p: (jnp.minimum(g, each - 1), 0)
        return lambda g, *p: (jnp.maximum(g - each, 0), 0)

    def place(g):
        if sides == 1:
            return starts[0] // step + g
        return jnp.where(g < each, starts[0] // step + g, starts[1] // step + g - each)

    in_specs = [
        pl.BlockSpec((step * slots * blk, blk), of_side(s)) for _ in range(count) for s in range(sides)
    ]
    in_specs += [
        pl.BlockSpec(
            (1, inner_width, blk, BJ * blk), functools.partial(lambda o, g, c, *p: (c[o], 0, 0, 0), o)
        )
        for o in offsets
    ]
    operands = [cycle, *index, *(array for piece in left for array in piece), *([right] * count)]
    aliases = {}
    if total is not None:
        in_specs.append(pl.BlockSpec((step, blk, BJ * blk), lambda g, *p: (place(g), 0, 0)))
        operands.append(total)
        aliases = {len(operands) - 1: 0}
    out_shape = jax.ShapeDtypeStruct((rows, blk, BJ * blk), jnp.float32)
    out_spec = pl.BlockSpec((step, blk, BJ * blk), lambda g, *p: (place(g), 0, 0))
    return pl.pallas_call(
        functools.partial(
            product_kernel, offsets, sides, starts, total is not None, step
        ),
        out_shape=out_shape,
        grid_spec=pltpu.PrefetchScalarGridSpec(
            num_scalar_prefetch=1 + count,
            grid=(each * sides,),
            in_specs=in_specs,
            out_specs=out_spec,
            scratch_shapes=[pltpu.VMEM((count, step * slots * blk, blk), jnp.bfloat16)] * (sides - 1),
        ),
        input_output_aliases=aliases,
        compiler_params=pltpu.CompilerParams(vmem_limit_bytes=VMEM_LIMIT),
        name="product",
        cost_estimate=pl.CostEstimate(flops=0, bytes_accessed=0, transcendentals=0),
    )(*operands)


def finish_kernel(parts, offset, cycle_ref, index_ref, right, total, *refs):
    out_ref, staged, sems = refs[-3:]
    arrays = refs[: len(refs) - 3]
    slots, blk = index_ref.shape[0], right.shape[2]
    wide = 2 * blk
    index, piece = index_ref[...], cycle_ref[...][0, offset]
    copies = []
    for at, (row, places) in enumerate(parts):
        inner = [index[s, row] for s in range(slots)]
        factor = []
        for s, (array, start) in enumerate(places):
            filled = jnp.where(inner[s] >= 0, 1.0, 0.0).astype(jnp.bfloat16)
            factor.append(arrays[array][start : start + blk, :] * filled)
        factor = jnp.concatenate(factor, axis=1)
        for c in range(BJ // 2):
            columns = slice(c * wide, (c + 1) * wide)
            rows_of = jnp.concatenate(
                [right[piece, jnp.maximum(k, 0), :, columns] for k in inner], axis=0
            )
            term = jnp.dot(factor, rows_of, preferred_element_type=jnp.float32)
            result = (total[row, :, columns] + term).astype(jnp.bfloat16)
            for j in range(2):
                staged[at, c * 2 + j] = result[:, j * blk : (j + 1) * blk]
        copies.append(pltpu.make_async_copy(staged.at[at], out_ref.at[row, 0], sems.at[at]))
        copies[-1].start()
    for copy in copies:
        copy.wait()


def finish(parts, cycle, offset, index, right, total, arrays, target):
    rows, blk = total.shape[0], total.shape[1]
    whole = pl.BlockSpec(memory_space=pltpu.VMEM)
    operands = [cycle[None], index, right, total, *arrays]
    in_specs = [whole] * len(operands)
    aliases = {}
    if target is not None:
        in_specs.append(pl.BlockSpec(memory_space=pl.ANY))
        operands.append(target)
        aliases = {len(operands) - 1: 0}
    return pl.pallas_call(
        functools.partial(finish_kernel, parts, offset),
        out_shape=jax.ShapeDtypeStruct((rows, 1, BJ, blk, blk), jnp.bfloat16),
        in_specs=in_specs,
        out_specs=pl.BlockSpec(memory_space=pl.ANY),
        scratch_shapes=[
            pltpu.VMEM((len(parts), BJ, blk, blk), jnp.bfloat16),
            pltpu.SemaphoreType.DMA((len(parts),)),
        ],
        input_output_aliases=aliases,
        compiler_params=pltpu.CompilerParams(vmem_limit_bytes=VMEM_LIMIT // 2),
        name="finish",
        cost_estimate=pl.CostEstimate(flops=0, bytes_accessed=0, transcendentals=0),
    )(*operands)


def pack_kernel(flat_ref, index_hbm, low_ref, high_ref, index_ref, wide_ref, sems):
    cut = flat_ref.shape[0] // 2
    index_copy = pltpu.make_async_copy(index_hbm, index_ref, sems.at[2])
    index_copy.start()
    copies = [
        pltpu.make_async_copy(
            flat_ref.at[pl.ds(h * cut, cut)], half_ref.at[pl.ds(0, cut)], sems.at[h]
        )
        for h, half_ref in enumerate((low_ref, high_ref))
    ]
    for copy in copies:
        copy.start()
    index_copy.wait()
    wide_ref[...] = jnp.zeros(wide_ref.shape, jnp.float32)
    wide_ref[: index_ref.shape[0], : index_ref.shape[1]] = index_ref[...].astype(jnp.float32)
    note = wide_ref[...].astype(jnp.bfloat16)
    for half_ref in (low_ref, high_ref):
        half_ref[cut:] = note
    for copy in copies:
        copy.wait()


def pack(flat, index):
    size, blk = flat.shape
    half = pltpu.VMEM((size // 2 + NOTE_ROWS, blk), jnp.bfloat16)
    return pl.pallas_call(
        pack_kernel,
        out_shape=(half, half),
        in_specs=[pl.BlockSpec(memory_space=pl.ANY)] * 2,
        out_specs=[pl.BlockSpec(memory_space=pltpu.VMEM)] * 2,
        scratch_shapes=[
            pltpu.VMEM(index.shape, jnp.int32),
            pltpu.VMEM((NOTE_ROWS, blk), jnp.float32),
            pltpu.SemaphoreType.DMA((3,)),
        ],
        compiler_params=pltpu.CompilerParams(vmem_limit_bytes=VMEM_LIMIT),
        name="pack",
        cost_estimate=pl.CostEstimate(flops=0, bytes_accessed=0, transcendentals=0),
    )(*(pltpu.with_memory_space_constraint(x, pltpu.HBM) for x in (flat, index)))


def body(a_values, a_index, b_values, b_index):
    n = lax.axis_size("row")
    order = ring_order(n)
    ahead = [(order[q], order[(q + 1) % n]) for q in range(n)]
    back = [(dst, src) for src, dst in ahead]
    whole_steps = n // 2 - 1
    rows, _, slots, blk, _ = a_values.shape
    half = rows // 2

    swap = [(0, 1), (1, 0)]
    flat = a_values.reshape(rows * slots * blk, blk)
    cut = half * slots * blk
    own_index = a_index[:, 0].T
    low_first, high_first = pack(flat, own_index)
    low_second, high_second = flat[:cut], flat[cut:]

    def read_note(message):
        return message[-NOTE_ROWS:][:slots, :rows].astype(jnp.int32)

    def move(array, way, name):
        with jax.named_scope(name):
            return lax.ppermute(array, "row", way)

    behind, beyond = [(low_first, high_second)], [(low_second, high_first)]

    def advance():
        low, high = behind[-1]
        far_low, far_high = beyond[-1]
        low, far_high = move(low, ahead, "low_ahead"), move(far_high, back, "high_back")
        high, far_low = move(high, ahead, "high_ahead"), move(far_low, back, "low_back")
        behind.append((low, high))
        beyond.append((far_low, far_high))

    advance()
    col = lax.axis_index("col")
    stored = b_values[:, 0]
    other, stored_index = lax.optimization_barrier((lax.ppermute(stored, "col", swap), b_index))
    stored_index = stored_index.reshape(-1)
    other_index = lax.ppermute(stored_index, "col", swap)
    inner_width = 2 * stored.shape[0] // n
    right = densify(col[None], stored_index, other_index, stored, other, n // 2, inner_width)

    around = np.array([[order[(order.index(r) + o) % n] for o in range(n)] for r in range(n)])
    cycle = lax.dynamic_index_in_dim(
        jnp.asarray(around, jnp.int32), lax.axis_index("row"), 0, keepdims=False
    )

    def after(done):
        low, far_high, done = lax.optimization_barrier((behind[-1][0], beyond[-1][1], done))
        behind[-1] = (low, behind[-1][1])
        beyond[-1] = (beyond[-1][0], far_high)
        return done


    total = None
    for k in range(1, whole_steps + 1):
        offsets, items = (n - k, k), [behind[k], beyond[k]]
        if k == 1:
            offsets, items = (0, *offsets), [(behind[0][0], beyond[0][1]), *items]
        if k < whole_steps:
            advance()
        else:
            per_row = slots * blk
            small, other_small = half // 4, 3 * half // 8
            low, high = behind[-1][0], beyond[-1][1]
            large_low = move(low[small * per_row :], ahead, "far_low_ahead")
            large_high = move(high[other_small * per_row : cut], back, "far_high_back")
        index = [read_note(behind[k][0]), read_note(beyond[k][1])]
        if k == 1:
            index.insert(0, own_index)
        total = product(cycle, offsets, index, items, right, total, (0, half), half, rows)
        if k < whole_steps:
            total = after(total)
    low, high = behind[-1][0][: small * per_row], beyond[-1][1][: other_small * per_row]
    small_low, small_high = move(low, ahead, "last_low_ahead"), move(high, back, "last_high_back")

    def blocks(array, first, stop, origin):
        return [
            (row, [(array, (row - origin) * per_row + s * blk) for s in range(slots)])
            for row in range(first, stop)
        ]

    far, far_index = n // 2, read_note(large_low)
    split = half + other_small
    parts = blocks(0, small, half, small) + blocks(1, split, rows, split)
    out = finish(parts, cycle, far, far_index, right, total, [large_low, large_high], None)
    parts = blocks(0, 0, small, 0) + blocks(1, half, split, half)
    out = finish(parts, cycle, far, far_index, right, total, [small_low, small_high], out)
    return out


def solution(mesh):
    placed = (
        P(("groups", "col"), "row", None, None, None),
        P(("groups", "col"), "row", None),
        P(("groups", "col"), "row", None, None, None),
        P(("groups", "col"), "row", None),
    )
    return jax.shard_map(
        body,
        mesh=mesh,
        in_specs=placed,
        out_specs=P(("groups", "col"), "row", None, None, None),
        check_vma=False,
    )
```

```python
import functools

import jax
import jax.numpy as jnp
import numpy as np
from jax import lax
from jax.experimental import pallas as pl
from jax.experimental.pallas import tpu as pltpu
from jax.sharding import PartitionSpec as P

BJ = 8
NOTE_ROWS = 16
VMEM_LIMIT = 20 * 1024 * 1024


def ring_order(n):
    if n == 8:
        return (0, 2, 4, 6, 7, 5, 3, 1)
    return tuple(range(n))


def densify_kernel(col_ref, own_index, other_index, own_ref, other_ref, dense_ref):
    source = pl.program_id(0)
    first = pl.program_id(1) * own_ref.shape[0]
    blk = own_ref.shape[-1]
    slots = own_ref.shape[1]
    for k in range(own_ref.shape[0]):
        stored = [
            jnp.where(source == 0, own_ref[k, t], other_ref[k, t]).astype(jnp.float32)
            for t in range(slots)
        ]
        at = [(first + k) * slots + t for t in range(slots)]
        columns = [jnp.where(source == 0, own_index[i], other_index[i]) for i in at]
        for j in range(BJ):
            total = jnp.zeros((blk, blk), jnp.float32)
            for t in range(slots):
                total = total + jnp.where(columns[t] == j, stored[t], 0.0)
            dense_ref[0, k, :, j * blk : (j + 1) * blk] = total.astype(jnp.bfloat16)


def densify(col, own_index, other_index, own, other, pieces, inner_width):
    slots, blk = own.shape[1], own.shape[-1]
    stored = (inner_width, slots, blk, blk)
    return pl.pallas_call(
        densify_kernel,
        out_shape=jax.ShapeDtypeStruct((2 * pieces, inner_width, blk, BJ * blk), jnp.bfloat16),
        grid_spec=pltpu.PrefetchScalarGridSpec(
            num_scalar_prefetch=3,
            grid=(2, pieces),
            in_specs=[
                pl.BlockSpec(stored, lambda s, g, c, *i: (jnp.where(s == 0, g, pieces - 1), 0, 0, 0)),
                pl.BlockSpec(stored, lambda s, g, c, *i: (jnp.where(s == 0, 0, g), 0, 0, 0)),
            ],
            out_specs=pl.BlockSpec(
                (1, inner_width, blk, BJ * blk),
                lambda s, g, c, *i: (jnp.where(s == 0, c[0], 1 - c[0]) * pieces + g, 0, 0, 0),
            ),
        ),
        compiler_params=pltpu.CompilerParams(vmem_limit_bytes=VMEM_LIMIT),
        name="densify",
        cost_estimate=pl.CostEstimate(flops=0, bytes_accessed=0, transcendentals=0),
    )(col, own_index, other_index, own, other)


def product_kernel(offsets, sides, starts, has_total, step, *refs):
    count = len(offsets)
    index = refs[1 : 1 + count]
    refs = refs[1 + count :]
    left = refs[: count * sides]
    right = refs[count * sides : count * (sides + 1)]
    rest = refs[count * (sides + 1) :]
    out_ref, held = (rest[-2], rest[-1]) if sides == 2 else (rest[-1], None)
    total_ref = rest[0] if has_total else None
    slots, blk = index[0].shape[0], left[0].shape[-1]
    wide = 2 * blk
    g = pl.program_id(0)
    if sides == 2:
        each = pl.num_programs(0) // 2
        second = g >= each
        row0 = jnp.where(second, starts[1] + (g - each) * step, starts[0] + g * step)
    else:
        row0 = starts[0] + g * step
    if sides == 2:
        for m in range(count):

            @pl.when(g < each)
            def _(m=m):
                held[m] = left[m * 2][...]

            @pl.when(g >= each)
            def _(m=m):
                held[m] = left[m * 2 + 1][...]

    for i in range(step):
        factors = []
        for m in range(count):
            inner = [index[m][s, row0 + i] for s in range(slots)]
            parts = []
            for s in range(slots):
                at = slice((i * slots + s) * blk, (i * slots + s + 1) * blk)
                part = left[m][at, :] if sides == 1 else held[m, at, :]
                parts.append(part * jnp.where(inner[s] >= 0, 1.0, 0.0).astype(jnp.bfloat16))
            factors.append((jnp.concatenate(parts, axis=1), [jnp.maximum(k, 0) for k in inner]))
        for c in range(BJ // 2):
            columns = slice(c * wide, (c + 1) * wide)
            total = total_ref[i, :, columns] if has_total else None
            for m in range(count):
                row, inner = factors[m]
                rows_of = jnp.concatenate([right[m][0, k, :, columns] for k in inner], axis=0)
                term = jnp.dot(row, rows_of, preferred_element_type=jnp.float32)
                total = term if total is None else total + term
            out_ref[i, :, columns] = total


def product(cycle, offsets, index, left, right, total, starts, size, rows, step=4):
    count, sides = len(offsets), len(starts)
    slots, blk = index[0].shape[0], left[0][0].shape[-1]
    each = size // step
    inner_width = right.shape[1]

    def of_side(s):
        if s == 0:
            return lambda g, *p: (jnp.minimum(g, each - 1), 0)
        return lambda g, *p: (jnp.maximum(g - each, 0), 0)

    def place(g):
        if sides == 1:
            return starts[0] // step + g
        return jnp.where(g < each, starts[0] // step + g, starts[1] // step + g - each)

    in_specs = [
        pl.BlockSpec((step * slots * blk, blk), of_side(s)) for _ in range(count) for s in range(sides)
    ]
    in_specs += [
        pl.BlockSpec(
            (1, inner_width, blk, BJ * blk), functools.partial(lambda o, g, c, *p: (c[o], 0, 0, 0), o)
        )
        for o in offsets
    ]
    operands = [cycle, *index, *(array for piece in left for array in piece), *([right] * count)]
    aliases = {}
    if total is not None:
        in_specs.append(pl.BlockSpec((step, blk, BJ * blk), lambda g, *p: (place(g), 0, 0)))
        operands.append(total)
        aliases = {len(operands) - 1: 0}
    out_shape = jax.ShapeDtypeStruct((rows, blk, BJ * blk), jnp.float32)
    out_spec = pl.BlockSpec((step, blk, BJ * blk), lambda g, *p: (place(g), 0, 0))
    return pl.pallas_call(
        functools.partial(
            product_kernel, offsets, sides, starts, total is not None, step
        ),
        out_shape=out_shape,
        grid_spec=pltpu.PrefetchScalarGridSpec(
            num_scalar_prefetch=1 + count,
            grid=(each * sides,),
            in_specs=in_specs,
            out_specs=out_spec,
            scratch_shapes=[pltpu.VMEM((count, step * slots * blk, blk), jnp.bfloat16)] * (sides - 1),
        ),
        input_output_aliases=aliases,
        compiler_params=pltpu.CompilerParams(vmem_limit_bytes=VMEM_LIMIT),
        name="product",
        cost_estimate=pl.CostEstimate(flops=0, bytes_accessed=0, transcendentals=0),
    )(*operands)


def finish_kernel(parts, offset, cycle_ref, index_ref, right, total, *refs):
    out_ref, staged, sems = refs[-3:]
    arrays = refs[: len(refs) - 3]
    slots, blk = index_ref.shape[0], right.shape[2]
    wide = 2 * blk
    index, piece = index_ref[...], cycle_ref[...][0, offset]
    copies = []
    for at, (row, places) in enumerate(parts):
        inner = [index[s, row] for s in range(slots)]
        factor = []
        for s, (array, start) in enumerate(places):
            filled = jnp.where(inner[s] >= 0, 1.0, 0.0).astype(jnp.bfloat16)
            factor.append(arrays[array][start : start + blk, :] * filled)
        factor = jnp.concatenate(factor, axis=1)
        for c in range(BJ // 2):
            columns = slice(c * wide, (c + 1) * wide)
            rows_of = jnp.concatenate(
                [right[piece, jnp.maximum(k, 0), :, columns] for k in inner], axis=0
            )
            term = jnp.dot(factor, rows_of, preferred_element_type=jnp.float32)
            result = (total[row, :, columns] + term).astype(jnp.bfloat16)
            for j in range(2):
                staged[at, c * 2 + j] = result[:, j * blk : (j + 1) * blk]
        copies.append(pltpu.make_async_copy(staged.at[at], out_ref.at[row, 0], sems.at[at]))
        copies[-1].start()
    for copy in copies:
        copy.wait()


def finish(parts, cycle, offset, index, right, total, arrays, target):
    rows, blk = total.shape[0], total.shape[1]
    whole = pl.BlockSpec(memory_space=pltpu.VMEM)
    operands = [cycle[None], index, right, total, *arrays]
    in_specs = [whole] * len(operands)
    aliases = {}
    if target is not None:
        in_specs.append(pl.BlockSpec(memory_space=pl.ANY))
        operands.append(target)
        aliases = {len(operands) - 1: 0}
    return pl.pallas_call(
        functools.partial(finish_kernel, parts, offset),
        out_shape=jax.ShapeDtypeStruct((rows, 1, BJ, blk, blk), jnp.bfloat16),
        in_specs=in_specs,
        out_specs=pl.BlockSpec(memory_space=pl.ANY),
        scratch_shapes=[
            pltpu.VMEM((len(parts), BJ, blk, blk), jnp.bfloat16),
            pltpu.SemaphoreType.DMA((len(parts),)),
        ],
        input_output_aliases=aliases,
        compiler_params=pltpu.CompilerParams(vmem_limit_bytes=VMEM_LIMIT // 2),
        name="finish",
        cost_estimate=pl.CostEstimate(flops=0, bytes_accessed=0, transcendentals=0),
    )(*operands)


def pack_kernel(flat_ref, index_hbm, low_ref, high_ref, index_ref, wide_ref, sems):
    cut = flat_ref.shape[0] // 2
    index_copy = pltpu.make_async_copy(index_hbm, index_ref, sems.at[2])
    index_copy.start()
    copies = [
        pltpu.make_async_copy(
            flat_ref.at[pl.ds(h * cut, cut)], half_ref.at[pl.ds(0, cut)], sems.at[h]
        )
        for h, half_ref in enumerate((low_ref, high_ref))
    ]
    for copy in copies:
        copy.start()
    index_copy.wait()
    wide_ref[...] = jnp.zeros(wide_ref.shape, jnp.float32)
    wide_ref[: index_ref.shape[0], : index_ref.shape[1]] = index_ref[...].astype(jnp.float32)
    note = wide_ref[...].astype(jnp.bfloat16)
    for half_ref in (low_ref, high_ref):
        half_ref[cut:] = note
    for copy in copies:
        copy.wait()


def pack(flat, index):
    size, blk = flat.shape
    half = pltpu.VMEM((size // 2 + NOTE_ROWS, blk), jnp.bfloat16)
    return pl.pallas_call(
        pack_kernel,
        out_shape=(half, half),
        in_specs=[pl.BlockSpec(memory_space=pl.ANY)] * 2,
        out_specs=[pl.BlockSpec(memory_space=pltpu.VMEM)] * 2,
        scratch_shapes=[
            pltpu.VMEM(index.shape, jnp.int32),
            pltpu.VMEM((NOTE_ROWS, blk), jnp.float32),
            pltpu.SemaphoreType.DMA((3,)),
        ],
        compiler_params=pltpu.CompilerParams(vmem_limit_bytes=VMEM_LIMIT),
        name="pack",
        cost_estimate=pl.CostEstimate(flops=0, bytes_accessed=0, transcendentals=0),
    )(*(pltpu.with_memory_space_constraint(x, pltpu.HBM) for x in (flat, index)))


def body(a_values, a_index, b_values, b_index):
    n = lax.axis_size("row")
    order = ring_order(n)
    ahead = [(order[q], order[(q + 1) % n]) for q in range(n)]
    back = [(dst, src) for src, dst in ahead]
    whole_steps = n // 2 - 1
    rows, _, slots, blk, _ = a_values.shape
    half = rows // 2

    swap = [(0, 1), (1, 0)]
    flat = a_values.reshape(rows * slots * blk, blk)
    cut = half * slots * blk
    own_index = a_index[:, 0].T
    low_first, high_first = pack(flat, own_index)
    low_first, high_first, b_values = lax.optimization_barrier((low_first, high_first, b_values))
    low_second, high_second = flat[:cut], flat[cut:]

    def read_note(message):
        return message[-NOTE_ROWS:][:slots, :rows].astype(jnp.int32)

    def move(array, way, name):
        with jax.named_scope(name):
            return lax.ppermute(array, "row", way)

    behind, beyond = [(low_first, high_second)], [(low_second, high_first)]

    def advance():
        low, high = behind[-1]
        far_low, far_high = beyond[-1]
        low, far_high = move(low, ahead, "low_ahead"), move(far_high, back, "high_back")
        high, far_low = move(high, ahead, "high_ahead"), move(far_low, back, "low_back")
        behind.append((low, high))
        beyond.append((far_low, far_high))

    advance()
    col = lax.axis_index("col")
    stored = b_values[:, 0]
    other, stored_index = lax.optimization_barrier((lax.ppermute(stored, "col", swap), b_index))
    stored_index = stored_index.reshape(-1)
    other_index = lax.ppermute(stored_index, "col", swap)
    inner_width = 2 * stored.shape[0] // n
    right = densify(col[None], stored_index, other_index, stored, other, n // 2, inner_width)

    around = np.array([[order[(order.index(r) + o) % n] for o in range(n)] for r in range(n)])
    cycle = lax.dynamic_index_in_dim(
        jnp.asarray(around, jnp.int32), lax.axis_index("row"), 0, keepdims=False
    )

    def after(done):
        low, far_high, done = lax.optimization_barrier((behind[-1][0], beyond[-1][1], done))
        behind[-1] = (low, behind[-1][1])
        beyond[-1] = (beyond[-1][0], far_high)
        return done


    total = None
    for k in range(1, whole_steps + 1):
        offsets, items = (n - k, k), [behind[k], beyond[k]]
        if k == 1:
            offsets, items = (0, *offsets), [(behind[0][0], beyond[0][1]), *items]
        if k < whole_steps:
            advance()
        else:
            small = half // 4
            at = small * slots * blk
            low, high = behind[-1][0], beyond[-1][1]
            large_parts = (
                small,
                half - small,
                move(low[at:], ahead, "far_low_ahead"),
                move(high[at:cut], back, "far_high_back"),
            )
        index = [read_note(behind[k][0]), read_note(beyond[k][1])]
        if k == 1:
            index.insert(0, own_index)
        total = product(cycle, offsets, index, items, right, total, (0, half), half, rows)
        if k < whole_steps:
            total = after(total)
    low, high = behind[-1][0][:at], beyond[-1][1][:at]
    small_parts = (0, small, move(low, ahead, "last_low_ahead"), move(high, back, "last_high_back"))
    last_parts = [large_parts, small_parts]
    out = None
    far_index = read_note(last_parts[0][2])
    per_row = slots * blk
    for start, size, low, high in last_parts:
        parts = [
            (h * half + start + i, [(h, i * per_row + s * blk) for s in range(slots)])
            for h in range(2)
            for i in range(size)
        ]
        out = finish(parts, cycle, n // 2, far_index, right, total, [low, high], out)
    return out


def solution(mesh):
    placed = (
        P(("groups", "col"), "row", None, None, None),
        P(("groups", "col"), "row", None),
        P(("groups", "col"), "row", None, None, None),
        P(("groups", "col"), "row", None),
    )
    return jax.shard_map(
        body,
        mesh=mesh,
        in_specs=placed,
        out_specs=P(("groups", "col"), "row", None, None, None),
        check_vma=False,
    )
```

```python
import functools

import jax
import jax.numpy as jnp
import numpy as np
from jax import lax
from jax.experimental import pallas as pl
from jax.experimental.pallas import tpu as pltpu
from jax.sharding import PartitionSpec as P

BJ = 8
NOTE_ROWS = 16
VMEM_LIMIT = 20 * 1024 * 1024


def ring_order(n):
    if n == 8:
        return (0, 2, 4, 6, 7, 5, 3, 1)
    return tuple(range(n))


def densify_kernel(col_ref, own_index, other_index, own_ref, other_ref, dense_ref):
    source = pl.program_id(0)
    first = pl.program_id(1) * own_ref.shape[0]
    blk = own_ref.shape[-1]
    slots = own_ref.shape[1]
    for k in range(own_ref.shape[0]):
        stored = [
            jnp.where(source == 0, own_ref[k, t], other_ref[k, t]).astype(jnp.float32)
            for t in range(slots)
        ]
        at = [(first + k) * slots + t for t in range(slots)]
        columns = [jnp.where(source == 0, own_index[i], other_index[i]) for i in at]
        for j in range(BJ):
            total = jnp.zeros((blk, blk), jnp.float32)
            for t in range(slots):
                total = total + jnp.where(columns[t] == j, stored[t], 0.0)
            dense_ref[0, k, :, j * blk : (j + 1) * blk] = total.astype(jnp.bfloat16)


def densify(col, own_index, other_index, own, other, pieces, inner_width):
    slots, blk = own.shape[1], own.shape[-1]
    stored = (inner_width, slots, blk, blk)
    return pl.pallas_call(
        densify_kernel,
        out_shape=jax.ShapeDtypeStruct((2 * pieces, inner_width, blk, BJ * blk), jnp.bfloat16),
        grid_spec=pltpu.PrefetchScalarGridSpec(
            num_scalar_prefetch=3,
            grid=(2, pieces),
            in_specs=[
                pl.BlockSpec(stored, lambda s, g, c, *i: (jnp.where(s == 0, g, pieces - 1), 0, 0, 0)),
                pl.BlockSpec(stored, lambda s, g, c, *i: (jnp.where(s == 0, 0, g), 0, 0, 0)),
            ],
            out_specs=pl.BlockSpec(
                (1, inner_width, blk, BJ * blk),
                lambda s, g, c, *i: (jnp.where(s == 0, c[0], 1 - c[0]) * pieces + g, 0, 0, 0),
            ),
        ),
        compiler_params=pltpu.CompilerParams(vmem_limit_bytes=VMEM_LIMIT),
        name="densify",
        cost_estimate=pl.CostEstimate(flops=0, bytes_accessed=0, transcendentals=0),
    )(col, own_index, other_index, own, other)


def product_kernel(offsets, sides, starts, has_total, step, *refs):
    count = len(offsets)
    index = refs[1 : 1 + count]
    refs = refs[1 + count :]
    left = refs[: count * sides]
    right = refs[count * sides : count * (sides + 1)]
    rest = refs[count * (sides + 1) :]
    out_ref, held = (rest[-2], rest[-1]) if sides == 2 else (rest[-1], None)
    total_ref = rest[0] if has_total else None
    slots, blk = index[0].shape[0], left[0].shape[-1]
    wide = 2 * blk
    g = pl.program_id(0)
    if sides == 2:
        each = pl.num_programs(0) // 2
        second = g >= each
        row0 = jnp.where(second, starts[1] + (g - each) * step, starts[0] + g * step)
    else:
        row0 = starts[0] + g * step
    if sides == 2:
        for m in range(count):

            @pl.when(g < each)
            def _(m=m):
                held[m] = left[m * 2][...]

            @pl.when(g >= each)
            def _(m=m):
                held[m] = left[m * 2 + 1][...]

    for i in range(step):
        factors = []
        for m in range(count):
            inner = [index[m][s, row0 + i] for s in range(slots)]
            parts = []
            for s in range(slots):
                at = slice((i * slots + s) * blk, (i * slots + s + 1) * blk)
                part = left[m][at, :] if sides == 1 else held[m, at, :]
                parts.append(part * jnp.where(inner[s] >= 0, 1.0, 0.0).astype(jnp.bfloat16))
            factors.append((jnp.concatenate(parts, axis=1), [jnp.maximum(k, 0) for k in inner]))
        for c in range(BJ // 2):
            columns = slice(c * wide, (c + 1) * wide)
            total = total_ref[i, :, columns] if has_total else None
            for m in range(count):
                row, inner = factors[m]
                rows_of = jnp.concatenate([right[m][0, k, :, columns] for k in inner], axis=0)
                term = jnp.dot(row, rows_of, preferred_element_type=jnp.float32)
                total = term if total is None else total + term
            out_ref[i, :, columns] = total


def product(cycle, offsets, index, left, right, total, starts, size, rows, step=4):
    count, sides = len(offsets), len(starts)
    slots, blk = index[0].shape[0], left[0][0].shape[-1]
    each = size // step
    inner_width = right.shape[1]

    def of_side(s):
        if s == 0:
            return lambda g, *p: (jnp.minimum(g, each - 1), 0)
        return lambda g, *p: (jnp.maximum(g - each, 0), 0)

    def place(g):
        if sides == 1:
            return starts[0] // step + g
        return jnp.where(g < each, starts[0] // step + g, starts[1] // step + g - each)

    in_specs = [
        pl.BlockSpec((step * slots * blk, blk), of_side(s)) for _ in range(count) for s in range(sides)
    ]
    in_specs += [
        pl.BlockSpec(
            (1, inner_width, blk, BJ * blk), functools.partial(lambda o, g, c, *p: (c[o], 0, 0, 0), o)
        )
        for o in offsets
    ]
    operands = [cycle, *index, *(array for piece in left for array in piece), *([right] * count)]
    aliases = {}
    if total is not None:
        in_specs.append(pl.BlockSpec((step, blk, BJ * blk), lambda g, *p: (place(g), 0, 0)))
        operands.append(total)
        aliases = {len(operands) - 1: 0}
    out_shape = jax.ShapeDtypeStruct((rows, blk, BJ * blk), jnp.float32)
    out_spec = pl.BlockSpec((step, blk, BJ * blk), lambda g, *p: (place(g), 0, 0))
    return pl.pallas_call(
        functools.partial(
            product_kernel, offsets, sides, starts, total is not None, step
        ),
        out_shape=out_shape,
        grid_spec=pltpu.PrefetchScalarGridSpec(
            num_scalar_prefetch=1 + count,
            grid=(each * sides,),
            in_specs=in_specs,
            out_specs=out_spec,
            scratch_shapes=[pltpu.VMEM((count, step * slots * blk, blk), jnp.bfloat16)] * (sides - 1),
        ),
        input_output_aliases=aliases,
        compiler_params=pltpu.CompilerParams(vmem_limit_bytes=VMEM_LIMIT),
        name="product",
        cost_estimate=pl.CostEstimate(flops=0, bytes_accessed=0, transcendentals=0),
    )(*operands)


def finish_kernel(parts, offset, cycle_ref, index_ref, right, total, *refs):
    out_ref, staged, sems = refs[-3:]
    arrays = refs[: len(refs) - 3]
    slots, blk = index_ref.shape[0], right.shape[2]
    wide = 2 * blk
    index, piece = index_ref[...], cycle_ref[...][0, offset]
    copies = []
    for at, (row, places) in enumerate(parts):
        inner = [index[s, row] for s in range(slots)]
        factor = []
        for s, (array, start) in enumerate(places):
            filled = jnp.where(inner[s] >= 0, 1.0, 0.0).astype(jnp.bfloat16)
            factor.append(arrays[array][start : start + blk, :] * filled)
        factor = jnp.concatenate(factor, axis=1)
        for c in range(BJ // 2):
            columns = slice(c * wide, (c + 1) * wide)
            rows_of = jnp.concatenate(
                [right[piece, jnp.maximum(k, 0), :, columns] for k in inner], axis=0
            )
            term = jnp.dot(factor, rows_of, preferred_element_type=jnp.float32)
            result = (total[row, :, columns] + term).astype(jnp.bfloat16)
            for j in range(2):
                staged[at, c * 2 + j] = result[:, j * blk : (j + 1) * blk]
        copies.append(pltpu.make_async_copy(staged.at[at], out_ref.at[row, 0], sems.at[at]))
        copies[-1].start()
    for copy in copies:
        copy.wait()


def finish(parts, cycle, offset, index, right, total, arrays, target):
    rows, blk = total.shape[0], total.shape[1]
    whole = pl.BlockSpec(memory_space=pltpu.VMEM)
    operands = [cycle[None], index, right, total, *arrays]
    in_specs = [whole] * len(operands)
    aliases = {}
    if target is not None:
        in_specs.append(pl.BlockSpec(memory_space=pl.ANY))
        operands.append(target)
        aliases = {len(operands) - 1: 0}
    return pl.pallas_call(
        functools.partial(finish_kernel, parts, offset),
        out_shape=jax.ShapeDtypeStruct((rows, 1, BJ, blk, blk), jnp.bfloat16),
        in_specs=in_specs,
        out_specs=pl.BlockSpec(memory_space=pl.ANY),
        scratch_shapes=[
            pltpu.VMEM((len(parts), BJ, blk, blk), jnp.bfloat16),
            pltpu.SemaphoreType.DMA((len(parts),)),
        ],
        input_output_aliases=aliases,
        compiler_params=pltpu.CompilerParams(vmem_limit_bytes=VMEM_LIMIT // 2),
        name="finish",
        cost_estimate=pl.CostEstimate(flops=0, bytes_accessed=0, transcendentals=0),
    )(*operands)


def pack_kernel(flat_ref, index_hbm, low_ref, high_ref, index_ref, wide_ref, sems):
    cut = flat_ref.shape[0] // 2
    index_copy = pltpu.make_async_copy(index_hbm, index_ref, sems.at[2])
    index_copy.start()
    copies = [
        pltpu.make_async_copy(
            flat_ref.at[pl.ds(h * cut, cut)], half_ref.at[pl.ds(0, cut)], sems.at[h]
        )
        for h, half_ref in enumerate((low_ref, high_ref))
    ]
    for copy in copies:
        copy.start()
    index_copy.wait()
    wide_ref[...] = jnp.zeros(wide_ref.shape, jnp.float32)
    wide_ref[: index_ref.shape[0], : index_ref.shape[1]] = index_ref[...].astype(jnp.float32)
    note = wide_ref[...].astype(jnp.bfloat16)
    for half_ref in (low_ref, high_ref):
        half_ref[cut:] = note
    for copy in copies:
        copy.wait()


def pack(flat, index):
    size, blk = flat.shape
    half = pltpu.VMEM((size // 2 + NOTE_ROWS, blk), jnp.bfloat16)
    return pl.pallas_call(
        pack_kernel,
        out_shape=(half, half),
        in_specs=[pl.BlockSpec(memory_space=pl.ANY)] * 2,
        out_specs=[pl.BlockSpec(memory_space=pltpu.VMEM)] * 2,
        scratch_shapes=[
            pltpu.VMEM(index.shape, jnp.int32),
            pltpu.VMEM((NOTE_ROWS, blk), jnp.float32),
            pltpu.SemaphoreType.DMA((3,)),
        ],
        compiler_params=pltpu.CompilerParams(vmem_limit_bytes=VMEM_LIMIT),
        name="pack",
        cost_estimate=pl.CostEstimate(flops=0, bytes_accessed=0, transcendentals=0),
    )(*(pltpu.with_memory_space_constraint(x, pltpu.HBM) for x in (flat, index)))


def body(a_values, a_index, b_values, b_index):
    n = lax.axis_size("row")
    order = ring_order(n)
    ahead = [(order[q], order[(q + 1) % n]) for q in range(n)]
    back = [(dst, src) for src, dst in ahead]
    whole_steps = n // 2 - 1
    rows, _, slots, blk, _ = a_values.shape
    half = rows // 2

    swap = [(0, 1), (1, 0)]
    flat = a_values.reshape(rows * slots * blk, blk)
    cut = half * slots * blk
    own_index = a_index[:, 0].T
    low_first, high_first = pack(flat, own_index)
    low_first, high_first, b_values = lax.optimization_barrier((low_first, high_first, b_values))
    low_second, high_second = flat[:cut], flat[cut:]

    def read_note(message):
        return message[-NOTE_ROWS:][:slots, :rows].astype(jnp.int32)

    def move(array, way, name):
        with jax.named_scope(name):
            return lax.ppermute(array, "row", way)

    behind, beyond = [(low_first, high_second)], [(low_second, high_first)]

    def advance():
        low, high = behind[-1]
        far_low, far_high = beyond[-1]
        low, far_high = move(low, ahead, "low_ahead"), move(far_high, back, "high_back")
        high, far_low = move(high, ahead, "high_ahead"), move(far_low, back, "low_back")
        behind.append((low, high))
        beyond.append((far_low, far_high))

    advance()
    col = lax.axis_index("col")
    stored = b_values[:, 0]
    other, stored_index = lax.optimization_barrier((lax.ppermute(stored, "col", swap), b_index))
    stored_index = stored_index.reshape(-1)
    other_index = lax.ppermute(stored_index, "col", swap)
    inner_width = 2 * stored.shape[0] // n
    right = densify(col[None], stored_index, other_index, stored, other, n // 2, inner_width)

    around = np.array([[order[(order.index(r) + o) % n] for o in range(n)] for r in range(n)])
    cycle = lax.dynamic_index_in_dim(
        jnp.asarray(around, jnp.int32), lax.axis_index("row"), 0, keepdims=False
    )

    def after(done):
        low, far_high, done = lax.optimization_barrier((behind[-1][0], beyond[-1][1], done))
        behind[-1] = (low, behind[-1][1])
        beyond[-1] = (beyond[-1][0], far_high)
        return done


    total = None
    for k in range(1, whole_steps + 1):
        offsets, items = (n - k, k), [behind[k], beyond[k]]
        if k == 1:
            offsets, items = (0, *offsets), [(behind[0][0], beyond[0][1]), *items]
        if k < whole_steps:
            advance()
        else:
            per_row = slots * blk
            small, other_small = half // 4, 3 * half // 8
            low, high = behind[-1][0], beyond[-1][1]
            large_low = move(low[small * per_row :], ahead, "far_low_ahead")
            large_high = move(high[other_small * per_row : cut], back, "far_high_back")
        index = [read_note(behind[k][0]), read_note(beyond[k][1])]
        if k == 1:
            index.insert(0, own_index)
        total = product(cycle, offsets, index, items, right, total, (0, half), half, rows)
        if k < whole_steps:
            total = after(total)
    low, high = behind[-1][0][: small * per_row], beyond[-1][1][: other_small * per_row]
    small_low, small_high = move(low, ahead, "last_low_ahead"), move(high, back, "last_high_back")

    def blocks(array, first, stop, origin):
        return [
            (row, [(array, (row - origin) * per_row + s * blk) for s in range(slots)])
            for row in range(first, stop)
        ]

    far, far_index = n // 2, read_note(large_low)
    split = half + other_small
    parts = blocks(0, small, half, small) + blocks(1, split, rows, split)
    out = finish(parts, cycle, far, far_index, right, total, [large_low, large_high], None)
    parts = blocks(0, 0, small, 0) + blocks(1, half, split, half)
    out = finish(parts, cycle, far, far_index, right, total, [small_low, small_high], out)
    return out


def solution(mesh):
    placed = (
        P(("groups", "col"), "row", None, None, None),
        P(("groups", "col"), "row", None),
        P(("groups", "col"), "row", None, None, None),
        P(("groups", "col"), "row", None),
    )
    return jax.shard_map(
        body,
        mesh=mesh,
        in_specs=placed,
        out_specs=P(("groups", "col"), "row", None, None, None),
        check_vma=False,
    )
```

```python
import functools

import jax
import jax.numpy as jnp
import numpy as np
from jax import lax
from jax.experimental import pallas as pl
from jax.experimental.pallas import tpu as pltpu
from jax.sharding import PartitionSpec as P

BJ = 8
NOTE_ROWS = 16
VMEM_LIMIT = 20 * 1024 * 1024


def ring_order(n):
    if n == 8:
        return (0, 2, 4, 6, 7, 5, 3, 1)
    return tuple(range(n))


def densify_kernel(col_ref, own_index, other_index, own_ref, other_ref, dense_ref):
    source = pl.program_id(0)
    first = pl.program_id(1) * own_ref.shape[0]
    blk = own_ref.shape[-1]
    slots = own_ref.shape[1]
    for k in range(own_ref.shape[0]):
        stored = [
            jnp.where(source == 0, own_ref[k, t], other_ref[k, t]).astype(jnp.float32)
            for t in range(slots)
        ]
        at = [(first + k) * slots + t for t in range(slots)]
        columns = [jnp.where(source == 0, own_index[i], other_index[i]) for i in at]
        for j in range(BJ):
            total = jnp.zeros((blk, blk), jnp.float32)
            for t in range(slots):
                total = total + jnp.where(columns[t] == j, stored[t], 0.0)
            dense_ref[0, k, :, j * blk : (j + 1) * blk] = total.astype(jnp.bfloat16)


def densify(col, own_index, other_index, own, other, pieces, inner_width):
    slots, blk = own.shape[1], own.shape[-1]
    stored = (inner_width, slots, blk, blk)
    return pl.pallas_call(
        densify_kernel,
        out_shape=jax.ShapeDtypeStruct((2 * pieces, inner_width, blk, BJ * blk), jnp.bfloat16),
        grid_spec=pltpu.PrefetchScalarGridSpec(
            num_scalar_prefetch=3,
            grid=(2, pieces),
            in_specs=[
                pl.BlockSpec(stored, lambda s, g, c, *i: (jnp.where(s == 0, g, pieces - 1), 0, 0, 0)),
                pl.BlockSpec(stored, lambda s, g, c, *i: (jnp.where(s == 0, 0, g), 0, 0, 0)),
            ],
            out_specs=pl.BlockSpec(
                (1, inner_width, blk, BJ * blk),
                lambda s, g, c, *i: (jnp.where(s == 0, c[0], 1 - c[0]) * pieces + g, 0, 0, 0),
            ),
        ),
        compiler_params=pltpu.CompilerParams(vmem_limit_bytes=VMEM_LIMIT),
        name="densify",
        cost_estimate=pl.CostEstimate(flops=0, bytes_accessed=0, transcendentals=0),
    )(col, own_index, other_index, own, other)


def product_kernel(offsets, sides, starts, has_total, step, *refs):
    count = len(offsets)
    index = refs[1 : 1 + count]
    refs = refs[1 + count :]
    left = refs[: count * sides]
    right = refs[count * sides : count * (sides + 1)]
    rest = refs[count * (sides + 1) :]
    out_ref, held = (rest[-2], rest[-1]) if sides == 2 else (rest[-1], None)
    total_ref = rest[0] if has_total else None
    slots, blk = index[0].shape[0], left[0].shape[-1]
    wide = 2 * blk
    g = pl.program_id(0)
    if sides == 2:
        each = pl.num_programs(0) // 2
        second = g >= each
        row0 = jnp.where(second, starts[1] + (g - each) * step, starts[0] + g * step)
    else:
        row0 = starts[0] + g * step
    if sides == 2:
        for m in range(count):

            @pl.when(g < each)
            def _(m=m):
                held[m] = left[m * 2][...]

            @pl.when(g >= each)
            def _(m=m):
                held[m] = left[m * 2 + 1][...]

    for i in range(step):
        factors = []
        for m in range(count):
            inner = [index[m][s, row0 + i] for s in range(slots)]
            parts = []
            for s in range(slots):
                at = slice((i * slots + s) * blk, (i * slots + s + 1) * blk)
                part = left[m][at, :] if sides == 1 else held[m, at, :]
                parts.append(part * jnp.where(inner[s] >= 0, 1.0, 0.0).astype(jnp.bfloat16))
            factors.append((jnp.concatenate(parts, axis=1), [jnp.maximum(k, 0) for k in inner]))
        for c in range(BJ // 2):
            columns = slice(c * wide, (c + 1) * wide)
            total = total_ref[i, :, columns] if has_total else None
            for m in range(count):
                row, inner = factors[m]
                rows_of = jnp.concatenate([right[m][0, k, :, columns] for k in inner], axis=0)
                term = jnp.dot(row, rows_of, preferred_element_type=jnp.float32)
                total = term if total is None else total + term
            out_ref[i, :, columns] = total


def product(cycle, offsets, index, left, right, total, starts, size, rows, step=4):
    count, sides = len(offsets), len(starts)
    slots, blk = index[0].shape[0], left[0][0].shape[-1]
    each = size // step
    inner_width = right.shape[1]

    def of_side(s):
        if s == 0:
            return lambda g, *p: (jnp.minimum(g, each - 1), 0)
        return lambda g, *p: (jnp.maximum(g - each, 0), 0)

    def place(g):
        if sides == 1:
            return starts[0] // step + g
        return jnp.where(g < each, starts[0] // step + g, starts[1] // step + g - each)

    in_specs = [
        pl.BlockSpec((step * slots * blk, blk), of_side(s)) for _ in range(count) for s in range(sides)
    ]
    in_specs += [
        pl.BlockSpec(
            (1, inner_width, blk, BJ * blk), functools.partial(lambda o, g, c, *p: (c[o], 0, 0, 0), o)
        )
        for o in offsets
    ]
    operands = [cycle, *index, *(array for piece in left for array in piece), *([right] * count)]
    aliases = {}
    if total is not None:
        in_specs.append(pl.BlockSpec((step, blk, BJ * blk), lambda g, *p: (place(g), 0, 0)))
        operands.append(total)
        aliases = {len(operands) - 1: 0}
    out_shape = jax.ShapeDtypeStruct((rows, blk, BJ * blk), jnp.float32)
    out_spec = pl.BlockSpec((step, blk, BJ * blk), lambda g, *p: (place(g), 0, 0))
    return pl.pallas_call(
        functools.partial(
            product_kernel, offsets, sides, starts, total is not None, step
        ),
        out_shape=out_shape,
        grid_spec=pltpu.PrefetchScalarGridSpec(
            num_scalar_prefetch=1 + count,
            grid=(each * sides,),
            in_specs=in_specs,
            out_specs=out_spec,
            scratch_shapes=[pltpu.VMEM((count, step * slots * blk, blk), jnp.bfloat16)] * (sides - 1),
        ),
        input_output_aliases=aliases,
        compiler_params=pltpu.CompilerParams(vmem_limit_bytes=VMEM_LIMIT),
        name="product",
        cost_estimate=pl.CostEstimate(flops=0, bytes_accessed=0, transcendentals=0),
    )(*operands)


def finish_kernel(parts, offset, cycle_ref, index_ref, right, total, *refs):
    out_ref, staged, sems = refs[-3:]
    arrays = refs[: len(refs) - 3]
    slots, blk = index_ref.shape[0], right.shape[2]
    wide = 2 * blk
    index, piece = index_ref[...], cycle_ref[...][0, offset]
    copies = []
    for at, (row, places) in enumerate(parts):
        inner = [index[s, row] for s in range(slots)]
        factor = []
        for s, (array, start) in enumerate(places):
            filled = jnp.where(inner[s] >= 0, 1.0, 0.0).astype(jnp.bfloat16)
            factor.append(arrays[array][start : start + blk, :] * filled)
        factor = jnp.concatenate(factor, axis=1)
        for c in range(BJ // 2):
            columns = slice(c * wide, (c + 1) * wide)
            rows_of = jnp.concatenate(
                [right[piece, jnp.maximum(k, 0), :, columns] for k in inner], axis=0
            )
            term = jnp.dot(factor, rows_of, preferred_element_type=jnp.float32)
            result = (total[row, :, columns] + term).astype(jnp.bfloat16)
            for j in range(2):
                staged[at, c * 2 + j] = result[:, j * blk : (j + 1) * blk]
            if c % 2 == 1:
                part = pl.ds(c * 2 - 2, 4)
                copies.append(
                    pltpu.make_async_copy(
                        staged.at[at, part], out_ref.at[row, 0, part], sems.at[at, c // 2]
                    )
                )
                copies[-1].start()
    for copy in copies:
        copy.wait()


def finish(parts, cycle, offset, index, right, total, arrays, target):
    rows, blk = total.shape[0], total.shape[1]
    whole = pl.BlockSpec(memory_space=pltpu.VMEM)
    operands = [cycle[None], index, right, total, *arrays]
    in_specs = [whole] * len(operands)
    aliases = {}
    if target is not None:
        in_specs.append(pl.BlockSpec(memory_space=pl.ANY))
        operands.append(target)
        aliases = {len(operands) - 1: 0}
    return pl.pallas_call(
        functools.partial(finish_kernel, parts, offset),
        out_shape=jax.ShapeDtypeStruct((rows, 1, BJ, blk, blk), jnp.bfloat16),
        in_specs=in_specs,
        out_specs=pl.BlockSpec(memory_space=pl.ANY),
        scratch_shapes=[
            pltpu.VMEM((len(parts), BJ, blk, blk), jnp.bfloat16),
            pltpu.SemaphoreType.DMA((len(parts), 2)),
        ],
        input_output_aliases=aliases,
        compiler_params=pltpu.CompilerParams(vmem_limit_bytes=VMEM_LIMIT // 2),
        name="finish",
        cost_estimate=pl.CostEstimate(flops=0, bytes_accessed=0, transcendentals=0),
    )(*operands)


def pack_kernel(flat_ref, index_hbm, low_ref, high_ref, index_ref, wide_ref, sems):
    cut = flat_ref.shape[0] // 2
    index_copy = pltpu.make_async_copy(index_hbm, index_ref, sems.at[2])
    index_copy.start()
    copies = [
        pltpu.make_async_copy(
            flat_ref.at[pl.ds(h * cut, cut)], half_ref.at[pl.ds(0, cut)], sems.at[h]
        )
        for h, half_ref in enumerate((low_ref, high_ref))
    ]
    for copy in copies:
        copy.start()
    index_copy.wait()
    wide_ref[...] = jnp.zeros(wide_ref.shape, jnp.float32)
    wide_ref[: index_ref.shape[0], : index_ref.shape[1]] = index_ref[...].astype(jnp.float32)
    note = wide_ref[...].astype(jnp.bfloat16)
    for half_ref in (low_ref, high_ref):
        half_ref[cut:] = note
    for copy in copies:
        copy.wait()


def pack(flat, index):
    size, blk = flat.shape
    half = pltpu.VMEM((size // 2 + NOTE_ROWS, blk), jnp.bfloat16)
    return pl.pallas_call(
        pack_kernel,
        out_shape=(half, half),
        in_specs=[pl.BlockSpec(memory_space=pl.ANY)] * 2,
        out_specs=[pl.BlockSpec(memory_space=pltpu.VMEM)] * 2,
        scratch_shapes=[
            pltpu.VMEM(index.shape, jnp.int32),
            pltpu.VMEM((NOTE_ROWS, blk), jnp.float32),
            pltpu.SemaphoreType.DMA((3,)),
        ],
        compiler_params=pltpu.CompilerParams(vmem_limit_bytes=VMEM_LIMIT),
        name="pack",
        cost_estimate=pl.CostEstimate(flops=0, bytes_accessed=0, transcendentals=0),
    )(*(pltpu.with_memory_space_constraint(x, pltpu.HBM) for x in (flat, index)))


def body(a_values, a_index, b_values, b_index):
    n = lax.axis_size("row")
    order = ring_order(n)
    ahead = [(order[q], order[(q + 1) % n]) for q in range(n)]
    back = [(dst, src) for src, dst in ahead]
    whole_steps = n // 2 - 1
    rows, _, slots, blk, _ = a_values.shape
    half = rows // 2

    swap = [(0, 1), (1, 0)]
    flat = a_values.reshape(rows * slots * blk, blk)
    cut = half * slots * blk
    own_index = a_index[:, 0].T
    low_first, high_first = pack(flat, own_index)
    low_first, high_first, b_values = lax.optimization_barrier((low_first, high_first, b_values))
    low_second, high_second = flat[:cut], flat[cut:]

    def read_note(message):
        return message[-NOTE_ROWS:][:slots, :rows].astype(jnp.int32)

    def move(array, way, name):
        with jax.named_scope(name):
            return lax.ppermute(array, "row", way)

    behind, beyond = [(low_first, high_second)], [(low_second, high_first)]

    def advance():
        low, high = behind[-1]
        far_low, far_high = beyond[-1]
        low, far_high = move(low, ahead, "low_ahead"), move(far_high, back, "high_back")
        high, far_low = move(high, ahead, "high_ahead"), move(far_low, back, "low_back")
        behind.append((low, high))
        beyond.append((far_low, far_high))

    advance()
    col = lax.axis_index("col")
    stored = b_values[:, 0]
    other, stored_index = lax.optimization_barrier((lax.ppermute(stored, "col", swap), b_index))
    stored_index = stored_index.reshape(-1)
    other_index = lax.ppermute(stored_index, "col", swap)
    inner_width = 2 * stored.shape[0] // n
    right = densify(col[None], stored_index, other_index, stored, other, n // 2, inner_width)

    around = np.array([[order[(order.index(r) + o) % n] for o in range(n)] for r in range(n)])
    cycle = lax.dynamic_index_in_dim(
        jnp.asarray(around, jnp.int32), lax.axis_index("row"), 0, keepdims=False
    )

    def after(done):
        low, far_high, done = lax.optimization_barrier((behind[-1][0], beyond[-1][1], done))
        behind[-1] = (low, behind[-1][1])
        beyond[-1] = (beyond[-1][0], far_high)
        return done


    total = None
    for k in range(1, whole_steps + 1):
        offsets, items = (n - k, k), [behind[k], beyond[k]]
        if k == 1:
            offsets, items = (0, *offsets), [(behind[0][0], beyond[0][1]), *items]
        if k < whole_steps:
            advance()
        else:
            small = half // 4
            at = small * slots * blk
            low, high = behind[-1][0], beyond[-1][1]
            large_parts = (
                small,
                half - small,
                move(low[at:], ahead, "far_low_ahead"),
                move(high[at:cut], back, "far_high_back"),
            )
        index = [read_note(behind[k][0]), read_note(beyond[k][1])]
        if k == 1:
            index.insert(0, own_index)
        total = product(cycle, offsets, index, items, right, total, (0, half), half, rows)
        if k < whole_steps:
            total = after(total)
    low, high = behind[-1][0][:at], beyond[-1][1][:at]
    small_parts = (0, small, move(low, ahead, "last_low_ahead"), move(high, back, "last_high_back"))
    last_parts = [large_parts, small_parts]
    out = None
    far_index = read_note(last_parts[0][2])
    per_row = slots * blk
    for start, size, low, high in last_parts:
        parts = [
            (h * half + start + i, [(h, i * per_row + s * blk) for s in range(slots)])
            for h in range(2)
            for i in range(size)
        ]
        out = finish(parts, cycle, n // 2, far_index, right, total, [low, high], out)
    return out


def solution(mesh):
    placed = (
        P(("groups", "col"), "row", None, None, None),
        P(("groups", "col"), "row", None),
        P(("groups", "col"), "row", None, None, None),
        P(("groups", "col"), "row", None),
    )
    return jax.shard_map(
        body,
        mesh=mesh,
        in_specs=placed,
        out_specs=P(("groups", "col"), "row", None, None, None),
        check_vma=False,
    )
```
